256 devices in a mesh: section: 32 (over z, x), dp: 4 (over y), expert: 2 (over core).
Axes of the slice: x: 4, y: 4, z: 8, core: 2. Of those that a mesh axis runs over, the one named last changes fastest.
Arguments:
- tokens: bfloat16 [32768, 1024], P(('section', 'dp', 'expert')), may hold values from -6 to 6
- expert_ids: int32 [32768, 8], P(('section', 'dp', 'expert')), may hold values from 0 to 31, all different within a row; in each aligned block of 128 rows (0 to 127, 128 to 255, ...) at most 40 rows name the same one
- probs: float32 [32768, 8], P(('section', 'dp', 'expert')), may hold values from 0.1 to 1
- first_weight: bfloat16 [32, 1024, 512], P('section'), may hold values from -0.1875 to 0.1875
- second_weight: bfloat16 [32, 512, 1024], P('section'), may hold values from -0.375 to 0.375
- upstream: bfloat16 [32768, 1024], P(('section', 'dp', 'expert')), may hold values from -6 to 6
Outputs:
- mixed: bfloat16 [32768, 1024], P(('section', 'dp', 'expert'))
- input_grad: bfloat16 [32768, 1024], P(('section', 'dp', 'expert'))
- second_grad: bfloat16 [32, 512, 1024], P('section', ('dp', 'expert'))
- prob_grad: float32 [32768, 8], P(('section', 'dp', 'expert'))
The draws below stay inside these ranges and needn't reach their ends.
Inputs may be any that keep to these rules, and one draw needn't show every extreme that they name: `expert_ids`: in each aligned block of 128 rows (one group's tokens), no expert is named by more than 40 rows, and in some block one expert is named by exactly 40 rows. The 8 experts of a row differ, and every expert is named somewhere.
All inputs are finite; a program needn't handle non-finite values.
Results may differ from the reference program's by a relative error of at most 0.0064.
Values may be sent and summed in bfloat16 or wider, within the bound.
A program may use at most 128 MiB of HBM per device.

```python
import math
import jax
import jax.numpy as jnp
import numpy as np
from jax import lax

MODEL_WIDTH = 1024
FF = 512
EXPERTS = 32
TOPK = 8
TOK_DEV = 128
REPLICAS = 8
TOKENS = 32768
SLOT_CAPACITY = 40
BUF_ROWS = 1280
N_SECTION = 32


def shard_levels(stream_key, dims, pieces, smallest, high):
    level = 1.0
    for axis_at, shards_of in pieces:
        heights = jax.random.uniform(jax.random.fold_in(jax.random.fold_in(stream_key, 6), axis_at), (shards_of,), jnp.float32, smallest / len(pieces), high / len(pieces))
        level = level * jnp.repeat(jnp.exp(heights), dims[axis_at] // shards_of).reshape((-1,) + (1,) * (len(dims) - 1 - axis_at))
    return level


def routed_block(own_key, own, number, rows, number_of, top, limit, slope):
    sequence = jax.random.permutation(own_key, number_of)
    heavy_load, usual = portions_of(number_of, rows * top, limit, slope, True), portions_of(number_of, rows * top, limit, slope, False)
    places = jnp.arange(number_of)

    def named(tallies, turn):
        used = int((tallies > 0).sum())
        fixed = max(1, used // 4)
        passed = fixed + (places - fixed + turn * (used - fixed)) % max(1, number_of - fixed)
        return jnp.zeros((number_of,), jnp.int32).at[sequence[jnp.where(places < fixed, places, passed)]].set(jnp.asarray(tallies, jnp.int32))

    tallies = jnp.where(number % 4 == 0, named(heavy_load, number // 4), named(usual, number - number // 4 - 1))
    mixed = jax.random.permutation(jax.random.fold_in(own, 3), number_of)
    donor, sink = mixed[0:number_of // 2 * 2:2], mixed[1:number_of // 2 * 2:2]
    slack = jnp.minimum(tallies[donor] - 1, limit - tallies[sink]) // 2
    slack = jnp.where((donor == sequence[0]) | (sink == sequence[0]) | (tallies[sink] == 0), 0, jnp.maximum(slack, 0))
    passed = jax.random.randint(jax.random.fold_in(own, 4), (number_of // 2,), 0, 1 << 20) % (slack + 1)
    tallies = tallies.at[donor].add(-passed).at[sink].add(passed)
    members = jnp.searchsorted(jnp.cumsum(tallies), jnp.arange(rows * top), side="right").astype(jnp.int32)
    listing = members.reshape(top, rows).T
    listing = listing[jax.random.permutation(jax.random.fold_in(own, 1), rows)]
    turn = jax.random.randint(jax.random.fold_in(own, 2), (rows, 1), 0, top)
    return jnp.take_along_axis(listing, (jnp.arange(top)[None, :] + turn) % top, axis=1)


def portions_of(number_of, total, limit, lean, full):
    portions = [(1 << 20) // math.isqrt(standing ** lean) + 1 for standing in range(1, number_of + 1)]
    largest = limit if full else min(limit, max(-(-total // number_of), total * portions[0] // sum(portions)))
    least = 1 if total - largest >= number_of - 1 else 0
    given, surplus = [largest] + [least] * (number_of - 1), total - largest - least * (number_of - 1)
    while surplus > 0:
        free = [i for i in range(1, number_of) if given[i] < largest] or [i for i in range(1, number_of) if given[i] < limit]
        whole, left = sum([portions[i] for i in free]), surplus
        for i in free:
            addition = min(limit - given[i], max(1, left * portions[i] // whole), surplus)
            given[i] = given[i] + addition
            surplus = surplus - addition
    return np.array(given)


def centred(own_key, extent, deviation, limit, cuts=(), kind=jnp.bfloat16):
    values = jax.random.normal(own_key, extent, jnp.float32) * deviation
    if len(cuts) > 0:
        values = shard_levels(own_key, extent, cuts, -0.22, 0.18) * values
    return jnp.clip(values, min=-limit, max=limit).astype(kind)


def setup_inputs(seed: int = 0) -> dict:
    arg_keys = jax.random.split(jax.random.key(seed), 7)
    tokens = centred(arg_keys[0], (TOKENS, MODEL_WIDTH), 1.0, 6.0, ((0, 256),))
    expert_ids_keys = jax.random.split(jax.random.fold_in(arg_keys[1], 1), TOKENS // TOK_DEV)
    expert_ids_turns = jax.random.permutation(jax.random.fold_in(arg_keys[1], 3), TOKENS // TOK_DEV)
    expert_ids = jax.vmap(lambda own, number: routed_block(jax.random.fold_in(arg_keys[1], 2), own, number, TOK_DEV, EXPERTS, TOPK, SLOT_CAPACITY, 2))(expert_ids_keys, expert_ids_turns).reshape((TOKENS, TOPK))
    probs = jnp.clip(0.1 + 0.9 * jax.random.uniform(arg_keys[2], (TOKENS, TOPK), jnp.float32) ** shard_levels(arg_keys[2], (TOKENS, TOPK), ((0, 256),), -0.2, 0.2), 0.1, 1.0)
    first_weight = centred(arg_keys[3], (EXPERTS, MODEL_WIDTH, FF), MODEL_WIDTH ** -0.5, 0.1875, ((0, 32),))
    second_weight = centred(arg_keys[4], (EXPERTS, FF, MODEL_WIDTH), (FF // 2) ** -0.5, 0.375, ((0, 32),))
    upstream = centred(arg_keys[5], (TOKENS, MODEL_WIDTH), 1.0, 6.0, ((0, 256),))
    return dict(tokens=tokens, expert_ids=expert_ids, probs=probs, first_weight=first_weight, second_weight=second_weight, upstream=upstream)


def silu_grad(value):
    sig = jax.nn.sigmoid(value)
    return sig * (1.0 + value * (1.0 - sig))

def expert_apply(operands):
    xrows, grows, first, second = operands
    pre_act = jnp.dot(xrows, first, preferred_element_type=jnp.float32)
    hidden = jax.nn.silu(pre_act).astype(jnp.bfloat16)
    expert_out = jnp.dot(hidden, second, preferred_element_type=jnp.float32).astype(jnp.bfloat16)
    weight_term = jnp.dot(hidden.T, grows, preferred_element_type=jnp.float32)
    hid_grad = jnp.dot(grows, second.T, preferred_element_type=jnp.float32)
    pre_grad = (hid_grad * silu_grad(pre_act)).astype(jnp.bfloat16)
    input_rows = jnp.dot(pre_grad, first.T, preferred_element_type=jnp.float32).astype(jnp.bfloat16)
    return (expert_out, input_rows, weight_term)

def reference(tokens, expert_ids, probs, first_weight, second_weight, upstream):
    tok_blocks = tokens.reshape(N_SECTION, REPLICAS, TOK_DEV, MODEL_WIDTH).transpose(1, 0, 2, 3)
    id_blocks = expert_ids.reshape(N_SECTION, REPLICAS, TOK_DEV * TOPK).transpose(1, 0, 2)
    prob_blocks = probs.reshape(N_SECTION, REPLICAS, TOK_DEV, TOPK).transpose(1, 0, 2, 3)
    up_blocks = upstream.reshape(N_SECTION, REPLICAS, TOK_DEV, MODEL_WIDTH).transpose(1, 0, 2, 3)

    def replica(carry, operands):
        tok_rows, id_rows, prob_rows, up_rows = operands
        onehot = (id_rows[:, :, None] == jnp.arange(EXPERTS, dtype=jnp.int32)[None, None, :]).astype(jnp.int32)
        before = jnp.cumsum(onehot, axis=1) - onehot
        slot_pos = lax.optimization_barrier(jnp.sum(before * onehot, axis=2))
        slot_rows = (jnp.arange(N_SECTION, dtype=jnp.int32)[:, None] * SLOT_CAPACITY + slot_pos).reshape(-1).astype(jnp.int32)
        chosen = id_rows.reshape(-1).astype(jnp.int32)
        doubled = jnp.repeat(tok_rows.reshape(N_SECTION * TOK_DEV, MODEL_WIDTH), TOPK, axis=0)
        xbuffer = jnp.zeros((EXPERTS, BUF_ROWS, MODEL_WIDTH), jnp.bfloat16).at[chosen, slot_rows].set(doubled)
        up_float = up_rows.astype(jnp.float32)
        scaled = (prob_rows[:, :, :, None] * up_float[:, :, None, :]).astype(jnp.bfloat16).reshape(N_SECTION * TOK_DEV * TOPK, MODEL_WIDTH)
        gbuffer = jnp.zeros((EXPERTS, BUF_ROWS, MODEL_WIDTH), jnp.bfloat16).at[chosen, slot_rows].set(scaled)
        expert_out, input_rows, weight_term = lax.map(expert_apply, (xbuffer, gbuffer, first_weight, second_weight))
        picked = expert_out[chosen, slot_rows].reshape(N_SECTION, TOK_DEV, TOPK, MODEL_WIDTH).astype(jnp.float32)
        mixed_rows = lax.optimization_barrier(jnp.sum(prob_rows[:, :, :, None] * picked, axis=2)).astype(jnp.bfloat16)
        prob_rows_grad = lax.optimization_barrier(jnp.sum(up_float[:, :, None, :] * picked, axis=3))
        back = input_rows[chosen, slot_rows].reshape(N_SECTION, TOK_DEV, TOPK, MODEL_WIDTH).astype(jnp.float32)
        grad_rows = lax.optimization_barrier(jnp.sum(back, axis=2)).astype(jnp.bfloat16)
        return (carry + weight_term, (mixed_rows, grad_rows, prob_rows_grad))
    start = jnp.zeros((EXPERTS, FF, MODEL_WIDTH), jnp.float32)
    total, outputs = lax.scan(replica, start, (tok_blocks, id_blocks, prob_blocks, up_blocks))
    mixed_blocks, grad_blocks, probg_blocks = outputs
    mixed = mixed_blocks.transpose(1, 0, 2, 3).reshape(TOKENS, MODEL_WIDTH)
    input_grad = grad_blocks.transpose(1, 0, 2, 3).reshape(TOKENS, MODEL_WIDTH)
    prob_grad = probg_blocks.transpose(1, 0, 2, 3).reshape(TOKENS, TOPK)
    second_grad = total.astype(jnp.bfloat16)
    return (mixed, input_grad, second_grad, prob_grad)
```

```python
import jax
import jax.numpy as jnp
from jax import lax
from jax.experimental import pallas as pl
from jax.experimental.pallas import tpu as pltpu
from jax.sharding import PartitionSpec as P

MESH = pl.DeviceIdType.MESH
F32 = jnp.float32
BF16 = jnp.bfloat16

NZ, NX, NY = 8, 4, 4
TOK = 128
D = 1024
FF = 512
TOPK = 8
HALF = D // 2
ROWS = NZ * TOK
BLOCK = 2 * TOK
NN = (((1,), (0,)), ((), ()))
NT = (((1,), (1,)), ((), ()))
TN = (((0,), (0,)), ((), ()))


def slot_of(offset):
    offset = offset % NZ
    if offset > NZ // 2:
        return 2 * (NZ - offset)
    return 2 * offset - 1 if offset else 0


def kernel(
    tok_in, up_in, w1_in, w2_in, ids, probs,
    mixed, igrad, sgrad, pgrad,
    tu, w1c, w2c, hid, hp, ps, part, rsb, rst,
    pts, ptr, pcs, pga, pgs, pgr,
    gown, gcs, gcr, gxa, gya, gyb, gxb, gs2,
    ag_s, ag_r, wx_s, wx_r, wy_s, wy_r, wc_s, wc_r, pt_s, pt_r, pg_s, pg_r,
    rs_s, rs_r, gc_s, gc_r, g1_s, g1_r, g2_s, g2_r, loc,
):
    section = lax.axis_index("section")
    y = lax.axis_index("dp")
    c = lax.axis_index("expert")
    z, x = section // NX, section % NX

    def at_z(j):
        return {"section": (z + j) % NZ * NX + x, "dp": y, "expert": c}

    def at_x(r):
        return {"section": z * NX + (x + r) % NX, "dp": y, "expert": c}

    def at_y(r):
        return {"section": section, "dp": (y + r) % NY, "expert": c}

    other_core = {"section": section, "dp": y, "expert": 1 - c}

    started = []

    def send(src, dst, s_sem, r_sem, device):
        copy = pltpu.make_async_remote_copy(
            src_ref=src, dst_ref=dst, send_sem=s_sem, recv_sem=r_sem,
            device_id=device, device_id_type=MESH,
        )
        copy.start()
        started.append(copy)

    def arrived(dst, s_sem, r_sem):
        pltpu.make_async_remote_copy(
            src_ref=dst, dst_ref=dst, send_sem=s_sem, recv_sem=r_sem,
            device_id=other_core, device_id_type=MESH,
        ).wait_recv()

    x_cols = pl.ds(pl.multiple_of(x * FF, FF), FF)
    local = [
        pltpu.make_async_copy(tok_in, tu.at[0, pl.ds(0, TOK)], loc.at[0]),
        pltpu.make_async_copy(up_in, tu.at[1, pl.ds(0, TOK)], loc.at[1]),
        pltpu.make_async_copy(w1_in.at[0], w1c.at[:, x_cols], loc.at[2]),
        pltpu.make_async_copy(w2_in.at[0], w2c.at[x_cols, :], loc.at[3]),
    ]
    for copy in local:
        copy.start()

    barrier = pltpu.get_barrier_semaphore()
    peers = [at_z(j) for j in range(1, NZ)] + [at_x(r) for r in range(1, NX)]
    peers += [at_y(r) for r in range(1, NY)] + [other_core]
    for peer in peers:
        pl.semaphore_signal(barrier, inc=1, device_id=peer, device_id_type=MESH)
    pl.semaphore_wait(barrier, len(peers))

    CH = TOK // 2
    sign = (1, -1)

    def ag_valid(h, d, a):
        return h <= 3 or (h == 4 and a == d)

    def ag_place(w, h, d, a):
        return tu.at[w, pl.ds(slot_of(-sign[d] * h) * TOK + a * CH, CH)]

    def ag_send(w, h, d, a):
        if h == 1:
            src = (tok_in, up_in)[w].at[pl.ds(a * CH, CH)]
        else:
            src = ag_place(w, h - 1, d, a)
        send(src, ag_place(w, h, d, a), ag_s.at[w, d, h - 1, a], ag_r.at[w, d, h - 1, a],
             at_z(sign[d]))

    def ag_hop(w, h):
        for a in range(2):
            for d in range(2):
                if ag_valid(h, d, a):
                    arrived(ag_place(w, h, d, a), ag_s.at[w, d, h - 1, a], ag_r.at[w, d, h - 1, a])
                    if h < 4 and ag_valid(h + 1, d, a):
                        ag_send(w, h + 1, d, a)

    q_mine = (y % 2) * 2 + c
    q_next = ((y + 1) % 2) * 2 + c
    q_core = (y % 2) * 2 + 1 - c
    q_both = ((y + 1) % 2) * 2 + 1 - c

    def w_place(w, e, q, part_of=None):
        rows = D // 4 if w == 0 else FF // 4
        base, size = q * rows, rows
        if part_of is not None:
            size = rows // 2
            base = base + part_of * size
        if w == 0:
            return w1c.at[pl.ds(pl.multiple_of(base, size), size),
                          pl.ds(pl.multiple_of(e * FF, FF), FF)]
        return w2c.at[pl.ds(pl.multiple_of(e * FF + base, size), size), :]

    def wx_send(w, r):
        rows = D // 4 if w == 0 else FF // 4
        src = (w1_in, w2_in)[w].at[0, pl.ds(pl.multiple_of(q_mine * rows, rows), rows), :]
        send(src, w_place(w, x, q_mine), wx_s.at[w, r - 1], wx_r.at[w, 3 - r], at_x(r))

    def wx_relay(w, r):
        e = (x + r) % NX
        arrived(w_place(w, e, q_mine), wx_s.at[w, r - 1], wx_r.at[w, r - 1])
        for k, step in ((0, 1), (1, -1)):
            send(w_place(w, e, q_mine, k), w_place(w, e, q_mine, k),
                 wy_s.at[w, r - 1, k], wy_r.at[w, r - 1, k], at_y(step))
        send(w_place(w, e, q_mine), w_place(w, e, q_mine),
             wc_s.at[w, r - 1, 0], wc_r.at[w, r - 1, 0], other_core)

    def wy_relay(w, r):
        e = (x + r) % NX
        for k in range(2):
            arrived(w_place(w, e, q_next, k), wy_s.at[w, r - 1, k], wy_r.at[w, r - 1, k])
        send(w_place(w, e, q_next), w_place(w, e, q_next),
             wc_s.at[w, r - 1, 1], wc_r.at[w, r - 1, 1], other_core)

    def w_arrive(w, r):
        e = (x + r) % NX
        arrived(w_place(w, e, q_core), wc_s.at[w, r - 1, 0], wc_r.at[w, r - 1, 0])
        arrived(w_place(w, e, q_both), wc_s.at[w, r - 1, 1], wc_r.at[w, r - 1, 1])

    for w in range(2):
        for a in range(2):
            for d in range(2):
                ag_send(w, 1, d, a)
        for r in (1, 3, 2):
            wx_send(w, r)

    lane = lax.broadcasted_iota(jnp.int32, (TOK, TOK), 1)
    table = jnp.zeros((TOK, TOK), F32)
    for k in range(TOPK):
        e = ids[:, k:k + 1]
        table += jnp.where(lane == (e >> 2) * 8 + (e & 3), probs[:, k:k + 1], 0.0)
    pts[...] = table.T[:NZ * 8]
    for j in range(1, NZ):
        there = slot_of(-j)
        send(pts.at[pl.ds(pl.multiple_of((z + j) % NZ * 8, 8), 8)], ptr.at[pl.ds(there * 8, 8)],
             pt_s.at[j - 1], pt_r.at[there - 1], at_z(j))
    ptr[0:8, :] = pts[pl.ds(pl.multiple_of(z * 8, 8), 8), :]
    pga[...] = jnp.zeros_like(pga)

    def columns(i):
        return pl.ds(pl.multiple_of(i * FF, FF), FF)

    def block_rows(b):
        return pl.ds(b * BLOCK, BLOCK)

    def pre_block(b):
        def one(i, carry):
            pre = lax.dot_general(tu[0, block_rows(b), :], w1c[:, columns(i)], NN,
                                  preferred_element_type=F32)
            p = jnp.concatenate(
                [jnp.sum(jnp.where(lane == (2 * b + k) * 8 + i, pcs[...], 0.0), axis=1,
                         keepdims=True) for k in range(2)], axis=0)
            sig = 1.0 / (1.0 + jnp.exp(-pre))
            act = pre * sig
            hid[block_rows(b), columns(i)] = act.astype(BF16)
            hp[block_rows(b), columns(i)] = (p * act).astype(BF16)
            ps[block_rows(b), columns(i)] = p * (sig * (1.0 + pre * (1.0 - sig)))
            return carry
        lax.fori_loop(0, NX, one, 0)

    def mixed_block(b):
        def one(n, carry):
            part[0, n, block_rows(b), :] = lax.dot_general(
                hp[block_rows(b), :], w2c[:, pl.ds(pl.multiple_of(n * HALF, HALF), HALF)], NN,
                preferred_element_type=F32)
            return carry
        lax.fori_loop(0, 2, one, 0)

    def back_block(b):
        def one(i, carry):
            dhu = lax.dot_general(tu[1, block_rows(b), :], w2c[columns(i), :], NT,
                                  preferred_element_type=F32)
            col = jnp.sum(hid[block_rows(b), columns(i)].astype(F32) * dhu, axis=1, keepdims=True)
            total = pga[...]
            for k in range(2):
                total += jnp.where(lane == (2 * b + k) * 8 + i, col[k * TOK:(k + 1) * TOK], 0.0)
            pga[...] = total
            hid[block_rows(b), columns(i)] = (dhu * ps[block_rows(b), columns(i)]).astype(BF16)
            return carry
        lax.fori_loop(0, NX, one, 0)

    def input_block(b):
        def one(n, carry):
            part[1, n, block_rows(b), :] = lax.dot_general(
                hid[block_rows(b), :], w1c[pl.ds(pl.multiple_of(n * HALF, HALF), HALF), :], NT,
                preferred_element_type=F32)
            return carry
        lax.fori_loop(0, 2, one, 0)

    def weight_grad(hf):
        def one(i, carry):
            g = lax.dot_general(hp[:, columns(i)], tu[1, :, hf * HALF:(hf + 1) * HALF], TN,
                                preferred_element_type=F32).reshape(NY, 2, FF // 8, HALF)
            mine = c == 0
            gown[hf, i] = jnp.where(mine, g[:, 0], g[:, 1])
            gcs[hf, i] = jnp.where(mine, g[:, 1], g[:, 0]).astype(BF16)
            return carry
        lax.fori_loop(0, NX, one, 0)
        send(gcs.at[hf], gcr.at[hf], gc_s.at[hf], gc_r.at[hf], other_core)

    def rs_rows(d, j):
        return pl.ds(slot_of(sign[d] * j) * TOK, TOK)

    def rs_send(w, d, j, n, src):
        send(src, rsb.at[w, d, j - 1, n], rs_s.at[w, d, j - 1, n], rs_r.at[w, d, j - 1, n],
             at_z(sign[d]))

    def rs_arrived(w, d, j, n):
        arrived(rsb.at[w, d, j, n], rs_s.at[w, d, j, n], rs_r.at[w, d, j, n])

    def rs_step(w, j):
        for d in range(2):
            if j == 4:
                rst[w, d] = part[w, d, rs_rows(d, j), :].astype(BF16)
                rs_send(w, d, j, d, rst.at[w, d])
        if j == 4:
            return
        for n in (1, 0) if j == 3 else (0, 1):
            for d in range(2):
                value = part[w, n, rs_rows(d, j), :]
                if j < 3 or n == d:
                    rs_arrived(w, d, j, n)
                    value = value + rsb[w, d, j, n].astype(F32)
                rsb[w, d, j, n] = value.astype(BF16)
                rs_send(w, d, j, n, rsb.at[w, d, j, n])

    def rs_end(w, out):
        for n in range(2):
            value = part[w, n, pl.ds(0, TOK), :]
            for d in range(2):
                rs_arrived(w, d, 0, n)
                value = value + rsb[w, d, 0, n].astype(F32)
            out[:, n * HALF:(n + 1) * HALF] = value.astype(BF16)

    def grad_first(hf):
        arrived(gcr.at[hf], gc_s.at[hf], gc_r.at[hf])

        def one(i, carry):
            gcr[hf, i] = (gown[hf, i] + gcr[hf, i].astype(F32)).astype(BF16)
            return carry
        lax.fori_loop(0, NX, one, 0)
        for r in (1, 3, 2):
            if hf == 0:
                send(gcr.at[0, (x + r) % NX], gxa.at[3 - r],
                     g1_s.at[0, r - 1], g1_r.at[0, 3 - r], at_x(r))
            else:
                send(gcr.at[1, :, (y + r) % NY], gyb.at[3 - r],
                     g1_s.at[1, r - 1], g1_r.at[1, 3 - r], at_y(r))

    def grad_second(hf):
        total = gcr[0, x].astype(F32) if hf == 0 else gcr[1, :, y].astype(F32)
        landed = gxa if hf == 0 else gyb
        for k in range(3):
            arrived(landed.at[k], g1_s.at[hf, k], g1_r.at[hf, k])
            total = total + landed[k].astype(F32)
        gs2[hf] = total.astype(BF16)
        for r in (1, 3, 2):
            if hf == 0:
                send(gs2.at[0, (y + r) % NY], gya.at[3 - r],
                     g2_s.at[0, r - 1], g2_r.at[0, 3 - r], at_y(r))
            else:
                send(gs2.at[1, (x + r) % NX], gxb.at[3 - r],
                     g2_s.at[1, r - 1], g2_r.at[1, 3 - r], at_x(r))

    def grad_end(hf):
        total = gs2[0, y].astype(F32) if hf == 0 else gs2[1, x].astype(F32)
        landed = gya if hf == 0 else gxb
        for k in range(3):
            arrived(landed.at[k], g2_s.at[hf, k], g2_r.at[hf, k])
            total = total + landed[k].astype(F32)
        sgrad[0, :, hf * HALF:(hf + 1) * HALF] = total.astype(BF16)

    ag_hop(0, 1)
    for r in (1, 3, 2):
        wx_relay(0, r)
    ag_hop(0, 2)
    for r in (1, 3, 2):
        wy_relay(0, r)
    for s in range(1, NZ):
        arrived(ptr.at[pl.ds(s * 8, 8)], pt_s.at[s - 1], pt_r.at[s - 1])
    pcs[...] = jnp.concatenate([ptr[...], jnp.zeros((TOK - NZ * 8, TOK), F32)], axis=0).T
    for copy in local:
        copy.wait()
    ag_hop(0, 3)
    for r in (1, 3, 2):
        w_arrive(0, r)
    pre_block(0)
    ag_hop(0, 4)
    for r in (1, 3, 2):
        wx_relay(1, r)
    pre_block(1)
    ag_hop(1, 1)
    for r in (1, 3, 2):
        wy_relay(1, r)
    pre_block(2)
    pre_block(3)
    ag_hop(1, 2)
    for r in (1, 3, 2):
        w_arrive(1, r)
    mixed_block(3)
    mixed_block(2)
    ag_hop(1, 3)
    rs_step(0, 4)
    mixed_block(1)
    mixed_block(0)
    ag_hop(1, 4)
    rs_step(0, 3)
    weight_grad(0)
    weight_grad(1)
    rs_step(0, 2)
    grad_first(0)
    grad_first(1)
    back_block(3)
    rs_step(0, 1)
    back_block(2)
    back_block(1)
    back_block(0)
    input_block(3)
    rs_step(1, 4)
    input_block(2)
    rs_step(1, 3)
    input_block(1)
    input_block(0)

    pgs[...] = pga[...].T[:NZ * 8]
    for j in range(1, NZ):
        send(pgs.at[pl.ds(slot_of(j) * 8, 8)], pgr.at[pl.ds(pl.multiple_of(z * 8, 8), 8)],
             pg_s.at[j - 1], pg_r.at[NZ - 1 - j], at_z(j))
    pgr[pl.ds(pl.multiple_of(z * 8, 8), 8), :] = pgs[0:8, :]

    grad_second(0)
    grad_second(1)
    rs_end(0, mixed)
    rs_step(1, 2)
    rs_step(1, 1)
    grad_end(0)
    grad_end(1)

    for j in range(1, NZ):
        arrived(pgr.at[pl.ds(pl.multiple_of((z + j) % NZ * 8, 8), 8)], pg_s.at[j - 1], pg_r.at[j - 1])
    table = jnp.concatenate([pgr[...], jnp.zeros((TOK - NZ * 8, TOK), F32)], axis=0).T
    out = jnp.zeros((TOK, TOPK), F32)
    place = lax.broadcasted_iota(jnp.int32, (TOK, TOPK), 1)
    for k in range(TOPK):
        e = ids[:, k:k + 1]
        col = jnp.sum(jnp.where(lane == (e >> 2) * 8 + (e & 3), table, 0.0), axis=1, keepdims=True)
        out += jnp.where(place == k, col, 0.0)
    pgrad[...] = out

    rs_end(1, igrad)
    for copy in started:
        copy.wait_send()


def body(tokens, expert_ids, probs, first_weight, second_weight, upstream):
    any_spec = pl.BlockSpec(memory_space=pl.ANY)
    vmem_spec = pl.BlockSpec(memory_space=pltpu.VMEM)
    dma = pltpu.SemaphoreType.DMA
    scratch = [
        pltpu.VMEM((2, ROWS, D), BF16),
        pltpu.VMEM((D, NX * FF), BF16),
        pltpu.VMEM((NX * FF, D), BF16),
        pltpu.VMEM((ROWS, NX * FF), BF16),
        pltpu.VMEM((ROWS, NX * FF), BF16),
        pltpu.VMEM((ROWS, NX * FF), F32),
        pltpu.VMEM((2, 2, ROWS, HALF), F32),
        pltpu.VMEM((2, 2, 4, 2, TOK, HALF), BF16),
        pltpu.VMEM((2, 2, TOK, HALF), BF16),
        pltpu.VMEM((NZ * 8, TOK), F32),
        pltpu.VMEM((NZ * 8, TOK), F32),
        pltpu.VMEM((TOK, TOK), F32),
        pltpu.VMEM((TOK, TOK), F32),
        pltpu.VMEM((NZ * 8, TOK), F32),
        pltpu.VMEM((NZ * 8, TOK), F32),
        pltpu.VMEM((2, NX, NY, FF // 8, HALF), F32),
        pltpu.VMEM((2, NX, NY, FF // 8, HALF), BF16),
        pltpu.VMEM((2, NX, NY, FF // 8, HALF), BF16),
        pltpu.VMEM((3, NY, FF // 8, HALF), BF16),
        pltpu.VMEM((3, FF // 8, HALF), BF16),
        pltpu.VMEM((3, NX, FF // 8, HALF), BF16),
        pltpu.VMEM((3, FF // 8, HALF), BF16),
        pltpu.VMEM((2, 4, FF // 8, HALF), BF16),
        dma((2, 2, 4, 2)), dma((2, 2, 4, 2)),
        dma((2, 3)), dma((2, 3)),
        dma((2, 3, 2)), dma((2, 3, 2)),
        dma((2, 3, 2)), dma((2, 3, 2)),
        dma((NZ - 1,)), dma((NZ - 1,)),
        dma((NZ - 1,)), dma((NZ - 1,)),
        dma((2, 2, 4, 2)), dma((2, 2, 4, 2)),
        dma((2,)), dma((2,)),
        dma((2, 3)), dma((2, 3)),
        dma((2, 3)), dma((2, 3)),
        dma((4,)),
    ]
    return pl.pallas_call(
        kernel,
        out_shape=(
            jax.ShapeDtypeStruct((TOK, D), BF16),
            jax.ShapeDtypeStruct((TOK, D), BF16),
            jax.ShapeDtypeStruct((1, FF // 8, D), BF16),
            jax.ShapeDtypeStruct((TOK, TOPK), F32),
        ),
        in_specs=[any_spec] * 4 + [vmem_spec] * 2,
        out_specs=(vmem_spec,) * 4,
        scratch_shapes=scratch,
        compiler_params=pltpu.CompilerParams(
            collective_id=0, has_side_effects=True, vmem_limit_bytes=60 * 1024 * 1024
        ),
        cost_estimate=pl.CostEstimate(
            flops=2 * 5 * ROWS * D * NX * FF, bytes_accessed=8 * 1024 * 1024,
            transcendentals=ROWS * NX * FF,
        ),
    )(tokens, upstream, first_weight, second_weight, expert_ids, probs)


def solution(mesh):
    everything = P(("section", "dp", "expert"), None)
    return jax.shard_map(
        body,
        mesh=mesh,
        in_specs=(everything, everything, everything, P("section", None, None),
                  P("section", None, None), everything),
        out_specs=(everything, everything, P("section", ("dp", "expert"), None), everything),
        check_vma=False,
    )
```

```python
import jax
import jax.numpy as jnp
from jax import lax
from jax.experimental import pallas as pl
from jax.experimental.pallas import tpu as pltpu
from jax.sharding import PartitionSpec as P

MESH = pl.DeviceIdType.MESH
F32 = jnp.float32
BF16 = jnp.bfloat16

NZ, NX, NY = 8, 4, 4
TOK = 128
D = 1024
FF = 512
TOPK = 8
HALF = D // 2
ROWS = NZ * TOK
BLOCK = 2 * TOK
NN = (((1,), (0,)), ((), ()))
NT = (((1,), (1,)), ((), ()))
TN = (((0,), (0,)), ((), ()))


def slot_of(offset):
    offset = offset % NZ
    if offset > NZ // 2:
        return 2 * (NZ - offset)
    return 2 * offset - 1 if offset else 0


def kernel(
    tok_in, up_in, w1_in, w2_in, ids, probs,
    mixed, igrad, sgrad, pgrad,
    tu, w1c, w2c, hid, hp, ps, part, rsb, rst,
    pts, ptr, pcs, pga, pgs, pgr,
    gown, gcs, gcr, gxa, gya, gyb, gxb, gs2,
    ag_s, ag_r, wx_s, wx_r, wy_s, wy_r, wc_s, wc_r, pt_s, pt_r, pg_s, pg_r,
    rs_s, rs_r, gc_s, gc_r, g1_s, g1_r, g2_s, g2_r, loc,
):
    section = lax.axis_index("section")
    y = lax.axis_index("dp")
    c = lax.axis_index("expert")
    z, x = section // NX, section % NX

    def at_z(j):
        return {"section": (z + j) % NZ * NX + x, "dp": y, "expert": c}

    def at_x(r):
        return {"section": z * NX + (x + r) % NX, "dp": y, "expert": c}

    def at_y(r):
        return {"section": section, "dp": (y + r) % NY, "expert": c}

    other_core = {"section": section, "dp": y, "expert": 1 - c}

    started = []

    def send(src, dst, s_sem, r_sem, device):
        copy = pltpu.make_async_remote_copy(
            src_ref=src, dst_ref=dst, send_sem=s_sem, recv_sem=r_sem,
            device_id=device, device_id_type=MESH,
        )
        copy.start()
        started.append(copy)

    def arrived(dst, s_sem, r_sem):
        pltpu.make_async_remote_copy(
            src_ref=dst, dst_ref=dst, send_sem=s_sem, recv_sem=r_sem,
            device_id=other_core, device_id_type=MESH,
        ).wait_recv()

    x_cols = pl.ds(pl.multiple_of(x * FF, FF), FF)
    local = [
        pltpu.make_async_copy(tok_in, tu.at[0, pl.ds(0, TOK)], loc.at[0]),
        pltpu.make_async_copy(up_in, tu.at[1, pl.ds(0, TOK)], loc.at[1]),
        pltpu.make_async_copy(w1_in.at[0], w1c.at[:, x_cols], loc.at[2]),
        pltpu.make_async_copy(w2_in.at[0], w2c.at[x_cols, :], loc.at[3]),
    ]
    for copy in local:
        copy.start()

    barrier = pltpu.get_barrier_semaphore()
    peers = [at_z(j) for j in range(1, NZ)] + [at_x(r) for r in range(1, NX)]
    peers += [at_y(r) for r in range(1, NY)] + [other_core]
    for peer in peers:
        pl.semaphore_signal(barrier, inc=1, device_id=peer, device_id_type=MESH)
    pl.semaphore_wait(barrier, len(peers))

    CH = TOK // 2
    sign = (1, -1)

    def ag_valid(h, d, a):
        return h <= 3 or (h == 4 and a == d)

    def ag_place(w, h, d, a):
        return tu.at[w, pl.ds(slot_of(-sign[d] * h) * TOK + a * CH, CH)]

    def ag_send(w, h, d, a):
        if h == 1:
            src = (tok_in, up_in)[w].at[pl.ds(a * CH, CH)]
        else:
            src = ag_place(w, h - 1, d, a)
        send(src, ag_place(w, h, d, a), ag_s.at[w, d, h - 1, a], ag_r.at[w, d, h - 1, a],
             at_z(sign[d]))

    def ag_hop(w, h):
        for a in range(2):
            for d in range(2):
                if ag_valid(h, d, a):
                    arrived(ag_place(w, h, d, a), ag_s.at[w, d, h - 1, a], ag_r.at[w, d, h - 1, a])
                    if h < 4 and ag_valid(h + 1, d, a):
                        ag_send(w, h + 1, d, a)

    q_mine = (y % 2) * 2 + c
    q_next = ((y + 1) % 2) * 2 + c
    q_core = (y % 2) * 2 + 1 - c
    q_both = ((y + 1) % 2) * 2 + 1 - c

    def w_place(w, e, q, part_of=None):
        rows = D // 4 if w == 0 else FF // 4
        base, size = q * rows, rows
        if part_of is not None:
            size = rows // 2
            base = base + part_of * size
        if w == 0:
            return w1c.at[pl.ds(pl.multiple_of(base, size), size),
                          pl.ds(pl.multiple_of(e * FF, FF), FF)]
        return w2c.at[pl.ds(pl.multiple_of(e * FF + base, size), size), :]

    def wx_send(w, r):
        rows = D // 4 if w == 0 else FF // 4
        src = (w1_in, w2_in)[w].at[0, pl.ds(pl.multiple_of(q_mine * rows, rows), rows), :]
        send(src, w_place(w, x, q_mine), wx_s.at[w, r - 1], wx_r.at[w, 3 - r], at_x(r))

    def wx_relay(w, r):
        e = (x + r) % NX
        arrived(w_place(w, e, q_mine), wx_s.at[w, r - 1], wx_r.at[w, r - 1])
        for k, step in ((0, 1), (1, -1)):
            send(w_place(w, e, q_mine, k), w_place(w, e, q_mine, k),
                 wy_s.at[w, r - 1, k], wy_r.at[w, r - 1, k], at_y(step))
        send(w_place(w, e, q_mine), w_place(w, e, q_mine),
             wc_s.at[w, r - 1, 0], wc_r.at[w, r - 1, 0], other_core)

    def wy_relay(w, r):
        e = (x + r) % NX
        for k in range(2):
            arrived(w_place(w, e, q_next, k), wy_s.at[w, r - 1, k], wy_r.at[w, r - 1, k])
        send(w_place(w, e, q_next), w_place(w, e, q_next),
             wc_s.at[w, r - 1, 1], wc_r.at[w, r - 1, 1], other_core)

    def w_arrive(w, r):
        e = (x + r) % NX
        arrived(w_place(w, e, q_core), wc_s.at[w, r - 1, 0], wc_r.at[w, r - 1, 0])
        arrived(w_place(w, e, q_both), wc_s.at[w, r - 1, 1], wc_r.at[w, r - 1, 1])

    for w in range(2):
        for a in range(2):
            for d in range(2):
                ag_send(w, 1, d, a)
        for r in (1, 3, 2):
            wx_send(w, r)

    lane = lax.broadcasted_iota(jnp.int32, (TOK, TOK), 1)
    place = lax.broadcasted_iota(jnp.int32, (NZ * 8, TOK), 0)

    def place_of(k):
        e = ids[k:k + 1, :]
        return (e >> 2) * 8 + (e & 3)

    table = jnp.zeros((NZ * 8, TOK), F32)
    for k in range(TOPK):
        table += jnp.where(place == place_of(k), probs[k:k + 1, :], 0.0)
    pts[...] = table
    for j in range(1, NZ):
        there = slot_of(-j)
        send(pts.at[pl.ds(pl.multiple_of((z + j) % NZ * 8, 8), 8)], ptr.at[pl.ds(there * 8, 8)],
             pt_s.at[j - 1], pt_r.at[there - 1], at_z(j))
    ptr[0:8, :] = pts[pl.ds(pl.multiple_of(z * 8, 8), 8), :]
    pga[...] = jnp.zeros_like(pga)

    def columns(i):
        return pl.ds(pl.multiple_of(i * FF, FF), FF)

    def block_rows(b):
        return pl.ds(b * BLOCK, BLOCK)

    def pre_block(b):
        def one(i, carry):
            pre = lax.dot_general(tu[0, block_rows(b), :], w1c[:, columns(i)], NN,
                                  preferred_element_type=F32)
            p = jnp.concatenate(
                [jnp.sum(jnp.where(lane == (2 * b + k) * 8 + i, pcs[...], 0.0), axis=1,
                         keepdims=True) for k in range(2)], axis=0)
            sig = 1.0 / (1.0 + jnp.exp(-pre))
            act = pre * sig
            hid[block_rows(b), columns(i)] = act.astype(BF16)
            hp[block_rows(b), columns(i)] = (p * act).astype(BF16)
            ps[block_rows(b), columns(i)] = p * (sig * (1.0 + pre * (1.0 - sig)))
            return carry
        lax.fori_loop(0, NX, one, 0)

    def mixed_block(b):
        def one(n, carry):
            part[0, n, block_rows(b), :] = lax.dot_general(
                hp[block_rows(b), :], w2c[:, pl.ds(pl.multiple_of(n * HALF, HALF), HALF)], NN,
                preferred_element_type=F32)
            return carry
        lax.fori_loop(0, 2, one, 0)

    def back_block(b):
        def one(i, carry):
            dhu = lax.dot_general(tu[1, block_rows(b), :], w2c[columns(i), :], NT,
                                  preferred_element_type=F32)
            col = jnp.sum(hid[block_rows(b), columns(i)].astype(F32) * dhu, axis=1, keepdims=True)
            total = pga[...]
            for k in range(2):
                total += jnp.where(lane == (2 * b + k) * 8 + i, col[k * TOK:(k + 1) * TOK], 0.0)
            pga[...] = total
            hid[block_rows(b), columns(i)] = (dhu * ps[block_rows(b), columns(i)]).astype(BF16)
            return carry
        lax.fori_loop(0, NX, one, 0)

    def input_block(b):
        def one(n, carry):
            part[1, n, block_rows(b), :] = lax.dot_general(
                hid[block_rows(b), :], w1c[pl.ds(pl.multiple_of(n * HALF, HALF), HALF), :], NT,
                preferred_element_type=F32)
            return carry
        lax.fori_loop(0, 2, one, 0)

    def weight_grad(hf):
        def one(i, carry):
            g = lax.dot_general(hp[:, columns(i)], tu[1, :, hf * HALF:(hf + 1) * HALF], TN,
                                preferred_element_type=F32).reshape(NY, 2, FF // 8, HALF)
            mine = c == 0
            gown[hf, i] = jnp.where(mine, g[:, 0], g[:, 1])
            gcs[hf, i] = jnp.where(mine, g[:, 1], g[:, 0]).astype(BF16)
            return carry
        lax.fori_loop(0, NX, one, 0)
        send(gcs.at[hf], gcr.at[hf], gc_s.at[hf], gc_r.at[hf], other_core)

    def rs_rows(d, j):
        return pl.ds(slot_of(sign[d] * j) * TOK, TOK)

    def rs_send(w, d, j, n, src):
        send(src, rsb.at[w, d, j - 1, n], rs_s.at[w, d, j - 1, n], rs_r.at[w, d, j - 1, n],
             at_z(sign[d]))

    def rs_arrived(w, d, j, n):
        arrived(rsb.at[w, d, j, n], rs_s.at[w, d, j, n], rs_r.at[w, d, j, n])

    def rs_step(w, j):
        for d in range(2):
            if j == 4:
                rst[w, d] = part[w, d, rs_rows(d, j), :].astype(BF16)
                rs_send(w, d, j, d, rst.at[w, d])
        if j == 4:
            return
        for n in (1, 0) if j == 3 else (0, 1):
            for d in range(2):
                value = part[w, n, rs_rows(d, j), :]
                if j < 3 or n == d:
                    rs_arrived(w, d, j, n)
                    value = value + rsb[w, d, j, n].astype(F32)
                rsb[w, d, j, n] = value.astype(BF16)
                rs_send(w, d, j, n, rsb.at[w, d, j, n])

    def rs_end(w, out):
        for n in range(2):
            value = part[w, n, pl.ds(0, TOK), :]
            for d in range(2):
                rs_arrived(w, d, 0, n)
                value = value + rsb[w, d, 0, n].astype(F32)
            out[:, n * HALF:(n + 1) * HALF] = value.astype(BF16)

    def grad_first(hf):
        arrived(gcr.at[hf], gc_s.at[hf], gc_r.at[hf])

        def one(i, carry):
            gcr[hf, i] = (gown[hf, i] + gcr[hf, i].astype(F32)).astype(BF16)
            return carry
        lax.fori_loop(0, NX, one, 0)
        for r in (1, 3, 2):
            if hf == 0:
                send(gcr.at[0, (x + r) % NX], gxa.at[3 - r],
                     g1_s.at[0, r - 1], g1_r.at[0, 3 - r], at_x(r))
            else:
                send(gcr.at[1, :, (y + r) % NY], gyb.at[3 - r],
                     g1_s.at[1, r - 1], g1_r.at[1, 3 - r], at_y(r))

    def grad_second(hf):
        total = gcr[0, x].astype(F32) if hf == 0 else gcr[1, :, y].astype(F32)
        landed = gxa if hf == 0 else gyb
        for k in range(3):
            arrived(landed.at[k], g1_s.at[hf, k], g1_r.at[hf, k])
            total = total + landed[k].astype(F32)
        gs2[hf] = total.astype(BF16)
        for r in (1, 3, 2):
            if hf == 0:
                send(gs2.at[0, (y + r) % NY], gya.at[3 - r],
                     g2_s.at[0, r - 1], g2_r.at[0, 3 - r], at_y(r))
            else:
                send(gs2.at[1, (x + r) % NX], gxb.at[3 - r],
                     g2_s.at[1, r - 1], g2_r.at[1, 3 - r], at_x(r))

    def grad_end(hf):
        total = gs2[0, y].astype(F32) if hf == 0 else gs2[1, x].astype(F32)
        landed = gya if hf == 0 else gxb
        for k in range(3):
            arrived(landed.at[k], g2_s.at[hf, k], g2_r.at[hf, k])
            total = total + landed[k].astype(F32)
        sgrad[0, :, hf * HALF:(hf + 1) * HALF] = total.astype(BF16)

    ag_hop(0, 1)
    for r in (1, 3, 2):
        wx_relay(0, r)
    ag_hop(0, 2)
    for s in range(1, NZ):
        arrived(ptr.at[pl.ds(s * 8, 8)], pt_s.at[s - 1], pt_r.at[s - 1])
    pcs[...] = jnp.concatenate([ptr[...], jnp.zeros((TOK - NZ * 8, TOK), F32)], axis=0).T
    for copy in local:
        copy.wait()
    ag_hop(1, 1)
    for r in (1, 3, 2):
        wy_relay(0, r)
    ag_hop(0, 3)
    for r in (1, 3, 2):
        wx_relay(1, r)
    for r in (1, 3, 2):
        w_arrive(0, r)
    ag_hop(1, 2)
    pre_block(0)
    ag_hop(0, 4)
    pre_block(1)
    ag_hop(1, 3)
    for r in (1, 3, 2):
        wy_relay(1, r)
    pre_block(3)
    pre_block(2)
    for r in (1, 3, 2):
        w_arrive(1, r)
    mixed_block(3)
    rs_step(0, 4)
    ag_hop(1, 4)
    mixed_block(2)
    rs_step(0, 3)
    back_block(3)
    input_block(3)
    rs_step(1, 4)
    mixed_block(1)
    rs_step(0, 2)
    back_block(2)
    input_block(2)
    rs_step(1, 3)
    mixed_block(0)
    rs_step(0, 1)
    weight_grad(0)
    weight_grad(1)
    back_block(1)
    input_block(1)
    rs_step(1, 2)
    grad_first(0)
    grad_first(1)
    back_block(0)
    input_block(0)
    rs_step(1, 1)

    pgs[...] = pga[...].T[:NZ * 8]
    for j in range(1, NZ):
        send(pgs.at[pl.ds(slot_of(j) * 8, 8)], pgr.at[pl.ds(pl.multiple_of(z * 8, 8), 8)],
             pg_s.at[j - 1], pg_r.at[NZ - 1 - j], at_z(j))
    pgr[pl.ds(pl.multiple_of(z * 8, 8), 8), :] = pgs[0:8, :]

    rs_end(0, mixed)
    grad_second(0)
    grad_second(1)
    grad_end(0)
    grad_end(1)

    for j in range(1, NZ):
        arrived(pgr.at[pl.ds(pl.multiple_of((z + j) % NZ * 8, 8), 8)], pg_s.at[j - 1], pg_r.at[j - 1])
    for k in range(TOPK):
        pgrad[k:k + 1, :] = jnp.sum(jnp.where(place == place_of(k), pgr[...], 0.0), axis=0,
                                    keepdims=True)

    rs_end(1, igrad)
    for copy in started:
        copy.wait_send()


def hand_over(a0, a1, a2, a3, b0, b1, b2, b3):
    for a, b in ((a0, b0), (a1, b1), (a2, b2), (a3, b3)):
        b[...] = a[...]


def body(tokens, expert_ids, probs, first_weight, second_weight, upstream):
    any_spec = pl.BlockSpec(memory_space=pl.ANY)
    vmem_spec = pl.BlockSpec(memory_space=pltpu.VMEM)
    dma = pltpu.SemaphoreType.DMA
    scratch = [
        pltpu.VMEM((2, ROWS, D), BF16),
        pltpu.VMEM((D, NX * FF), BF16),
        pltpu.VMEM((NX * FF, D), BF16),
        pltpu.VMEM((ROWS, NX * FF), BF16),
        pltpu.VMEM((ROWS, NX * FF), BF16),
        pltpu.VMEM((ROWS, NX * FF), F32),
        pltpu.VMEM((2, 2, ROWS, HALF), F32),
        pltpu.VMEM((2, 2, 4, 2, TOK, HALF), BF16),
        pltpu.VMEM((2, 2, TOK, HALF), BF16),
        pltpu.VMEM((NZ * 8, TOK), F32),
        pltpu.VMEM((NZ * 8, TOK), F32),
        pltpu.VMEM((TOK, TOK), F32),
        pltpu.VMEM((TOK, TOK), F32),
        pltpu.VMEM((NZ * 8, TOK), F32),
        pltpu.VMEM((NZ * 8, TOK), F32),
        pltpu.VMEM((2, NX, NY, FF // 8, HALF), F32),
        pltpu.VMEM((2, NX, NY, FF // 8, HALF), BF16),
        pltpu.VMEM((2, NX, NY, FF // 8, HALF), BF16),
        pltpu.VMEM((3, NY, FF // 8, HALF), BF16),
        pltpu.VMEM((3, FF // 8, HALF), BF16),
        pltpu.VMEM((3, NX, FF // 8, HALF), BF16),
        pltpu.VMEM((3, FF // 8, HALF), BF16),
        pltpu.VMEM((2, 4, FF // 8, HALF), BF16),
        dma((2, 2, 4, 2)), dma((2, 2, 4, 2)),
        dma((2, 3)), dma((2, 3)),
        dma((2, 3, 2)), dma((2, 3, 2)),
        dma((2, 3, 2)), dma((2, 3, 2)),
        dma((NZ - 1,)), dma((NZ - 1,)),
        dma((NZ - 1,)), dma((NZ - 1,)),
        dma((2, 2, 4, 2)), dma((2, 2, 4, 2)),
        dma((2,)), dma((2,)),
        dma((2, 3)), dma((2, 3)),
        dma((2, 3)), dma((2, 3)),
        dma((4,)),
    ]
    results = pl.pallas_call(
        kernel,
        out_shape=(
            jax.ShapeDtypeStruct((TOK, D), BF16),
            jax.ShapeDtypeStruct((TOK, D), BF16),
            jax.ShapeDtypeStruct((1, FF // 8, D), BF16),
            jax.ShapeDtypeStruct((TOPK, TOK), F32),
        ),
        in_specs=[any_spec] * 4 + [vmem_spec] * 2,
        out_specs=(vmem_spec,) * 4,
        scratch_shapes=scratch,
        compiler_params=pltpu.CompilerParams(
            collective_id=0, has_side_effects=True, vmem_limit_bytes=60 * 1024 * 1024
        ),
        cost_estimate=pl.CostEstimate(
            flops=2 * 5 * ROWS * D * NX * FF, bytes_accessed=8 * 1024 * 1024,
            transcendentals=ROWS * NX * FF,
        ),
    )(tokens, upstream, first_weight, second_weight, expert_ids.T, probs.T)
    mixed, igrad, sgrad, pgrad = pl.pallas_call(
        hand_over,
        out_shape=tuple(jax.ShapeDtypeStruct(r.shape, r.dtype) for r in results),
        in_specs=[vmem_spec] * 4,
        out_specs=(vmem_spec,) * 4,
    )(*results)
    return mixed, igrad, sgrad, pgrad.T


def solution(mesh):
    everything = P(("section", "dp", "expert"), None)
    return jax.shard_map(
        body,
        mesh=mesh,
        in_specs=(everything, everything, everything, P("section", None, None),
                  P("section", None, None), everything),
        out_specs=(everything, everything, P("section", ("dp", "expert"), None), everything),
        check_vma=False,
    )
```

```python
import jax
import jax.numpy as jnp
from jax import lax
from jax.experimental import pallas as pl
from jax.experimental.pallas import tpu as pltpu
from jax.sharding import PartitionSpec as P

MESH = pl.DeviceIdType.MESH
F32 = jnp.float32
BF16 = jnp.bfloat16

NZ, NX, NY = 8, 4, 4
TOK = 128
D = 1024
FF = 512
TOPK = 8
HALF = D // 2
ROWS = NZ * TOK
BLOCK = 2 * TOK
NN = (((1,), (0,)), ((), ()))
NT = (((1,), (1,)), ((), ()))
TN = (((0,), (0,)), ((), ()))


def slot_of(offset):
    offset = offset % NZ
    if offset > NZ // 2:
        return 2 * (NZ - offset)
    return 2 * offset - 1 if offset else 0


def kernel(
    tok_in, up_in, w1_in, w2_in, ids, probs,
    mixed, igrad, sgrad, pgrad,
    tu, w1c, w2c, hid, hp, ps, part, rsb, rst,
    pts, ptr, pcs, pga, pgs, pgr,
    gown, gcs, gcr, gxa, gya, gyb, gxb, gs2,
    ag_s, ag_r, wx_s, wx_r, wy_s, wy_r, wc_s, wc_r, pt_s, pt_r, pg_s, pg_r,
    rs_s, rs_r, gc_s, gc_r, g1_s, g1_r, g2_s, g2_r, loc,
):
    section = lax.axis_index("section")
    y = lax.axis_index("dp")
    c = lax.axis_index("expert")
    z, x = section // NX, section % NX

    def at_z(j):
        return {"section": (z + j) % NZ * NX + x, "dp": y, "expert": c}

    def at_x(r):
        return {"section": z * NX + (x + r) % NX, "dp": y, "expert": c}

    def at_y(r):
        return {"section": section, "dp": (y + r) % NY, "expert": c}

    other_core = {"section": section, "dp": y, "expert": 1 - c}

    started = []

    def send(src, dst, s_sem, r_sem, device):
        copy = pltpu.make_async_remote_copy(
            src_ref=src, dst_ref=dst, send_sem=s_sem, recv_sem=r_sem,
            device_id=device, device_id_type=MESH,
        )
        copy.start()
        started.append(copy)

    def arrived(dst, s_sem, r_sem):
        pltpu.make_async_remote_copy(
            src_ref=dst, dst_ref=dst, send_sem=s_sem, recv_sem=r_sem,
            device_id=other_core, device_id_type=MESH,
        ).wait_recv()

    x_cols = pl.ds(pl.multiple_of(x * FF, FF), FF)
    local = [
        pltpu.make_async_copy(tok_in, tu.at[0, pl.ds(0, TOK)], loc.at[0]),
        pltpu.make_async_copy(up_in, tu.at[1, pl.ds(0, TOK)], loc.at[1]),
        pltpu.make_async_copy(w1_in.at[0], w1c.at[:, x_cols], loc.at[2]),
        pltpu.make_async_copy(w2_in.at[0], w2c.at[x_cols, :], loc.at[3]),
    ]
    for copy in local:
        copy.start()

    barrier = pltpu.get_barrier_semaphore()
    peers = [at_z(j) for j in range(1, NZ)] + [at_x(r) for r in range(1, NX)]
    peers += [at_y(r) for r in range(1, NY)] + [other_core]
    for peer in peers:
        pl.semaphore_signal(barrier, inc=1, device_id=peer, device_id_type=MESH)
    pl.semaphore_wait(barrier, len(peers))

    CH = TOK // 2
    sign = (1, -1)

    def ag_valid(h, d, a):
        return h <= 3 or (h == 4 and a == d)

    def ag_place(w, h, d, a):
        return tu.at[w, pl.ds(slot_of(-sign[d] * h) * TOK + a * CH, CH)]

    def ag_send(w, h, d, a):
        if h == 1:
            src = (tok_in, up_in)[w].at[pl.ds(a * CH, CH)]
        else:
            src = ag_place(w, h - 1, d, a)
        send(src, ag_place(w, h, d, a), ag_s.at[w, d, h - 1, a], ag_r.at[w, d, h - 1, a],
             at_z(sign[d]))

    def ag_hop(w, h, *chunks):
        for a in chunks or (0, 1):
            for d in range(2):
                if ag_valid(h, d, a):
                    arrived(ag_place(w, h, d, a), ag_s.at[w, d, h - 1, a], ag_r.at[w, d, h - 1, a])
                    if h < 4 and ag_valid(h + 1, d, a):
                        ag_send(w, h + 1, d, a)

    q_mine = (y % 2) * 2 + c
    q_next = ((y + 1) % 2) * 2 + c
    q_core = (y % 2) * 2 + 1 - c
    q_both = ((y + 1) % 2) * 2 + 1 - c

    def w_place(w, e, q, part_of=None):
        rows = D // 4 if w == 0 else FF // 4
        base, size = q * rows, rows
        if part_of is not None:
            size = rows // 2
            base = base + part_of * size
        if w == 0:
            return w1c.at[pl.ds(pl.multiple_of(base, size), size),
                          pl.ds(pl.multiple_of(e * FF, FF), FF)]
        return w2c.at[pl.ds(pl.multiple_of(e * FF + base, size), size), :]

    def wx_send(w, r):
        rows = D // 4 if w == 0 else FF // 4
        src = (w1_in, w2_in)[w].at[0, pl.ds(pl.multiple_of(q_mine * rows, rows), rows), :]
        send(src, w_place(w, x, q_mine), wx_s.at[w, r - 1], wx_r.at[w, 3 - r], at_x(r))

    def wx_relay(w, r):
        e = (x + r) % NX
        arrived(w_place(w, e, q_mine), wx_s.at[w, r - 1], wx_r.at[w, r - 1])
        for k, step in ((0, 1), (1, -1)):
            send(w_place(w, e, q_mine, k), w_place(w, e, q_mine, k),
                 wy_s.at[w, r - 1, k], wy_r.at[w, r - 1, k], at_y(step))
        send(w_place(w, e, q_mine), w_place(w, e, q_mine),
             wc_s.at[w, r - 1, 0], wc_r.at[w, r - 1, 0], other_core)

    def wy_relay(w, r):
        e = (x + r) % NX
        for k in range(2):
            arrived(w_place(w, e, q_next, k), wy_s.at[w, r - 1, k], wy_r.at[w, r - 1, k])
        send(w_place(w, e, q_next), w_place(w, e, q_next),
             wc_s.at[w, r - 1, 1], wc_r.at[w, r - 1, 1], other_core)

    def w_arrive(w, r):
        e = (x + r) % NX
        arrived(w_place(w, e, q_core), wc_s.at[w, r - 1, 0], wc_r.at[w, r - 1, 0])
        arrived(w_place(w, e, q_both), wc_s.at[w, r - 1, 1], wc_r.at[w, r - 1, 1])

    for w in range(2):
        for a in range(2):
            for d in range(2):
                ag_send(w, 1, d, a)
        for r in (1, 3, 2):
            wx_send(w, r)

    lane = lax.broadcasted_iota(jnp.int32, (TOK, TOK), 1)
    place = lax.broadcasted_iota(jnp.int32, (NZ * 8, TOK), 0)

    def place_of(k):
        e = ids[k:k + 1, :]
        return (e >> 2) * 8 + (e & 3)

    table = jnp.zeros((NZ * 8, TOK), F32)
    for k in range(TOPK):
        table += jnp.where(place == place_of(k), probs[k:k + 1, :], 0.0)
    pts[...] = table
    for j in range(1, NZ):
        there = slot_of(-j)
        send(pts.at[pl.ds(pl.multiple_of((z + j) % NZ * 8, 8), 8)], ptr.at[pl.ds(there * 8, 8)],
             pt_s.at[j - 1], pt_r.at[there - 1], at_z(j))
    ptr[0:8, :] = pts[pl.ds(pl.multiple_of(z * 8, 8), 8), :]
    pga[...] = jnp.zeros_like(pga)

    def columns(i):
        return pl.ds(pl.multiple_of(i * FF, FF), FF)

    def pre_block(first, size, e_from=0, e_to=NX):
        rows = pl.ds(first * TOK, size * TOK)

        def one(i, carry):
            pre = lax.dot_general(tu[0, rows, :], w1c[:, columns(i)], NN,
                                  preferred_element_type=F32)
            p = jnp.concatenate(
                [jnp.sum(jnp.where(lane == (first + k) * 8 + i, pcs[...], 0.0), axis=1,
                         keepdims=True) for k in range(size)], axis=0)
            sig = 0.5 * jnp.tanh(0.5 * pre) + 0.5
            act = pre * sig
            hid[rows, columns(i)] = act.astype(BF16)
            hp[rows, columns(i)] = (p * act).astype(BF16)
            ps[rows, columns(i)] = p * (sig * (1.0 + pre * (1.0 - sig)))
            return carry
        lax.fori_loop(e_from, e_to, one, 0)

    def mixed_block(first, size):
        rows = pl.ds(first * TOK, size * TOK)

        def one(n, carry):
            part[0, n, rows, :] = lax.dot_general(hp[rows, :], w2c[:, columns(n)], NN,
                                                  preferred_element_type=F32)
            return carry
        lax.fori_loop(0, 2, one, 0)

    def back_block(first, size, e_from=0, e_to=NX):
        rows = pl.ds(first * TOK, size * TOK)

        def one(i, carry):
            dhu = lax.dot_general(tu[1, rows, :], w2c[columns(i), :], NT,
                                  preferred_element_type=F32)
            col = jnp.sum(hid[rows, columns(i)].astype(F32) * dhu, axis=1, keepdims=True)
            total = pga[...]
            for k in range(size):
                total += jnp.where(lane == (first + k) * 8 + i, col[k * TOK:(k + 1) * TOK], 0.0)
            pga[...] = total
            hid[rows, columns(i)] = (dhu * ps[rows, columns(i)]).astype(BF16)
            return carry
        lax.fori_loop(e_from, e_to, one, 0)

    def input_block(first, size):
        rows = pl.ds(first * TOK, size * TOK)

        def one(n, carry):
            part[1, n, rows, :] = lax.dot_general(hid[rows, :], w1c[columns(n), :], NT,
                                                  preferred_element_type=F32)
            return carry
        lax.fori_loop(0, 2, one, 0)

    def weight_grad(hf):
        def one(i, carry):
            g = lax.dot_general(hp[:, columns(i)], tu[1, :, hf * HALF:(hf + 1) * HALF], TN,
                                preferred_element_type=F32).reshape(NY, 2, FF // 8, HALF)
            mine = c == 0
            gown[hf, i] = jnp.where(mine, g[:, 0], g[:, 1])
            gcs[hf, i] = jnp.where(mine, g[:, 1], g[:, 0]).astype(BF16)
            return carry
        lax.fori_loop(0, NX, one, 0)
        send(gcs.at[hf], gcr.at[hf], gc_s.at[hf], gc_r.at[hf], other_core)

    def rs_rows(d, j):
        return pl.ds(slot_of(sign[d] * j) * TOK, TOK)

    def rs_send(w, d, j, n, src):
        send(src, rsb.at[w, d, j - 1, n], rs_s.at[w, d, j - 1, n], rs_r.at[w, d, j - 1, n],
             at_z(sign[d]))

    def rs_arrived(w, d, j, n):
        arrived(rsb.at[w, d, j, n], rs_s.at[w, d, j, n], rs_r.at[w, d, j, n])

    def rs_start(w):
        for d in range(2):
            rst[w, d] = part[w, d, rs_rows(d, 4), :].astype(BF16)
            rs_send(w, d, 4, d, rst.at[w, d])
        for d in range(2):
            rsb[w, d, 3, 1 - d] = part[w, 1 - d, rs_rows(d, 3), :].astype(BF16)
            rs_send(w, d, 3, 1 - d, rsb.at[w, d, 3, 1 - d])

    def rs_step(w, j):
        for n in range(2):
            for d in range(2):
                half = 1 - d if n == 0 else d
                if j == 3 and n == 0:
                    continue
                rs_arrived(w, d, j, half)
                value = part[w, half, rs_rows(d, j), :] + rsb[w, d, j, half].astype(F32)
                rsb[w, d, j, half] = value.astype(BF16)
                rs_send(w, d, j, half, rsb.at[w, d, j, half])

    def rs_end(w, out):
        for n in range(2):
            value = part[w, n, pl.ds(0, TOK), :]
            for d in range(2):
                rs_arrived(w, d, 0, n)
                value = value + rsb[w, d, 0, n].astype(F32)
            out[:, n * HALF:(n + 1) * HALF] = value.astype(BF16)

    def grad_first(hf):
        arrived(gcr.at[hf], gc_s.at[hf], gc_r.at[hf])

        def one(i, carry):
            gcr[hf, i] = (gown[hf, i] + gcr[hf, i].astype(F32)).astype(BF16)
            return carry
        lax.fori_loop(0, NX, one, 0)
        for r in (1, 3, 2):
            if hf == 0:
                send(gcr.at[0, (x + r) % NX], gxa.at[3 - r],
                     g1_s.at[0, r - 1], g1_r.at[0, 3 - r], at_x(r))
            else:
                send(gcr.at[1, :, (y + r) % NY], gyb.at[3 - r],
                     g1_s.at[1, r - 1], g1_r.at[1, 3 - r], at_y(r))

    def grad_second(hf):
        total = gcr[0, x].astype(F32) if hf == 0 else gcr[1, :, y].astype(F32)
        landed = gxa if hf == 0 else gyb
        for k in range(3):
            arrived(landed.at[k], g1_s.at[hf, k], g1_r.at[hf, k])
            total = total + landed[k].astype(F32)
        gs2[hf] = total.astype(BF16)
        for r in (1, 3, 2):
            if hf == 0:
                send(gs2.at[0, (y + r) % NY], gya.at[3 - r],
                     g2_s.at[0, r - 1], g2_r.at[0, 3 - r], at_y(r))
            else:
                send(gs2.at[1, (x + r) % NX], gxb.at[3 - r],
                     g2_s.at[1, r - 1], g2_r.at[1, 3 - r], at_x(r))

    def grad_end(hf):
        total = gs2[0, y].astype(F32) if hf == 0 else gs2[1, x].astype(F32)
        landed = gya if hf == 0 else gxb
        for k in range(3):
            arrived(landed.at[k], g2_s.at[hf, k], g2_r.at[hf, k])
            total = total + landed[k].astype(F32)
        sgrad[0, :, hf * HALF:(hf + 1) * HALF] = total.astype(BF16)

    def p_columns():
        for k in range(1, NZ):
            arrived(ptr.at[pl.ds(k * 8, 8)], pt_s.at[k - 1], pt_r.at[k - 1])
        pcs[...] = jnp.concatenate([ptr[...], jnp.zeros((TOK - NZ * 8, TOK), F32)], axis=0).T

    def p_back():
        pgs[...] = pga[...].T[:NZ * 8]
        for j in range(1, NZ):
            send(pgs.at[pl.ds(slot_of(j) * 8, 8)], pgr.at[pl.ds(pl.multiple_of(z * 8, 8), 8)],
                 pg_s.at[j - 1], pg_r.at[NZ - 1 - j], at_z(j))
        pgr[pl.ds(pl.multiple_of(z * 8, 8), 8), :] = pgs[0:8, :]

    def p_end():
        for j in range(1, NZ):
            arrived(pgr.at[pl.ds(pl.multiple_of((z + j) % NZ * 8, 8), 8)],
                    pg_s.at[j - 1], pg_r.at[j - 1])
        for k in range(TOPK):
            pgrad[k:k + 1, :] = jnp.sum(jnp.where(place == place_of(k), pgr[...], 0.0), axis=0,
                                        keepdims=True)

    def each(f, w):
        for r in (1, 3, 2):
            f(w, r)

    ag_hop(0, 1)
    each(wx_relay, 0)
    ag_hop(1, 1, 0)
    p_columns()
    for copy in local:
        copy.wait()
    ag_hop(1, 1, 1)
    each(wy_relay, 0)
    ag_hop(0, 2, 0)
    each(wx_relay, 1)
    ag_hop(0, 2, 1)
    each(w_arrive, 0)
    pre_block(0, 4, 0, 2)
    ag_hop(1, 2, 0)
    pre_block(0, 4, 2, 4)
    ag_hop(1, 2, 1)
    each(wy_relay, 1)
    ag_hop(0, 3, 0)
    ag_hop(0, 3, 1)
    each(w_arrive, 1)
    pre_block(4, 2)
    back_block(0, 4, 0, 1)
    ag_hop(1, 3, 0)
    back_block(0, 4, 1, 3)
    ag_hop(1, 3, 1)
    back_block(4, 2)
    mixed_block(4, 2)
    ag_hop(0, 4)
    pre_block(6, 2)
    mixed_block(6, 2)
    rs_start(0)
    input_block(4, 2)
    ag_hop(1, 4)
    back_block(6, 2)
    input_block(6, 2)
    rs_start(1)
    rs_step(0, 3)
    weight_grad(0)
    grad_first(0)
    mixed_block(0, 4)
    rs_step(0, 2)
    back_block(0, 4, 3, 4)
    rs_step(1, 3)
    weight_grad(1)
    input_block(0, 4)
    rs_step(0, 1)
    grad_first(1)
    rs_step(1, 2)
    p_back()
    grad_second(0)
    rs_step(1, 1)
    grad_second(1)
    rs_end(0, mixed)
    p_end()
    grad_end(0)
    grad_end(1)
    rs_end(1, igrad)
    for copy in started:
        copy.wait_send()


def hand_over(a0, a1, a2, a3, b0, b1, b2, b3):
    for a, b in ((a0, b0), (a1, b1), (a2, b2), (a3, b3)):
        b[...] = a[...]


def body(tokens, expert_ids, probs, first_weight, second_weight, upstream):
    any_spec = pl.BlockSpec(memory_space=pl.ANY)
    vmem_spec = pl.BlockSpec(memory_space=pltpu.VMEM)
    dma = pltpu.SemaphoreType.DMA
    scratch = [
        pltpu.VMEM((2, ROWS, D), BF16),
        pltpu.VMEM((D, NX * FF), BF16),
        pltpu.VMEM((NX * FF, D), BF16),
        pltpu.VMEM((ROWS, NX * FF), BF16),
        pltpu.VMEM((ROWS, NX * FF), BF16),
        pltpu.VMEM((ROWS, NX * FF), F32),
        pltpu.VMEM((2, 2, ROWS, HALF), F32),
        pltpu.VMEM((2, 2, 4, 2, TOK, HALF), BF16),
        pltpu.VMEM((2, 2, TOK, HALF), BF16),
        pltpu.VMEM((NZ * 8, TOK), F32),
        pltpu.VMEM((NZ * 8, TOK), F32),
        pltpu.VMEM((TOK, TOK), F32),
        pltpu.VMEM((TOK, TOK), F32),
        pltpu.VMEM((NZ * 8, TOK), F32),
        pltpu.VMEM((NZ * 8, TOK), F32),
        pltpu.VMEM((2, NX, NY, FF // 8, HALF), F32),
        pltpu.VMEM((2, NX, NY, FF // 8, HALF), BF16),
        pltpu.VMEM((2, NX, NY, FF // 8, HALF), BF16),
        pltpu.VMEM((3, NY, FF // 8, HALF), BF16),
        pltpu.VMEM((3, FF // 8, HALF), BF16),
        pltpu.VMEM((3, NX, FF // 8, HALF), BF16),
        pltpu.VMEM((3, FF // 8, HALF), BF16),
        pltpu.VMEM((2, 4, FF // 8, HALF), BF16),
        dma((2, 2, 4, 2)), dma((2, 2, 4, 2)),
        dma((2, 3)), dma((2, 3)),
        dma((2, 3, 2)), dma((2, 3, 2)),
        dma((2, 3, 2)), dma((2, 3, 2)),
        dma((NZ - 1,)), dma((NZ - 1,)),
        dma((NZ - 1,)), dma((NZ - 1,)),
        dma((2, 2, 4, 2)), dma((2, 2, 4, 2)),
        dma((2,)), dma((2,)),
        dma((2, 3)), dma((2, 3)),
        dma((2, 3)), dma((2, 3)),
        dma((4,)),
    ]
    results = pl.pallas_call(
        kernel,
        out_shape=(
            jax.ShapeDtypeStruct((TOK, D), BF16),
            jax.ShapeDtypeStruct((TOK, D), BF16),
            jax.ShapeDtypeStruct((1, FF // 8, D), BF16),
            jax.ShapeDtypeStruct((TOPK, TOK), F32),
        ),
        in_specs=[any_spec] * 4 + [vmem_spec] * 2,
        out_specs=(vmem_spec,) * 4,
        scratch_shapes=scratch,
        compiler_params=pltpu.CompilerParams(
            collective_id=0, has_side_effects=True, vmem_limit_bytes=60 * 1024 * 1024
        ),
        cost_estimate=pl.CostEstimate(
            flops=2 * 5 * ROWS * D * NX * FF, bytes_accessed=8 * 1024 * 1024,
            transcendentals=ROWS * NX * FF,
        ),
    )(tokens, upstream, first_weight, second_weight, expert_ids.T, probs.T)
    mixed, igrad, sgrad, pgrad = pl.pallas_call(
        hand_over,
        out_shape=tuple(jax.ShapeDtypeStruct(r.shape, r.dtype) for r in results),
        in_specs=[vmem_spec] * 4,
        out_specs=(vmem_spec,) * 4,
    )(*results)
    return mixed, igrad, sgrad, pgrad.T


def solution(mesh):
    everything = P(("section", "dp", "expert"), None)
    return jax.shard_map(
        body,
        mesh=mesh,
        in_specs=(everything, everything, everything, P("section", None, None),
                  P("section", None, None), everything),
        out_specs=(everything, everything, P("section", ("dp", "expert"), None), everything),
        check_vma=False,
    )
```

```python
import jax
import jax.numpy as jnp
from jax import lax
from jax.experimental import pallas as pl
from jax.experimental.pallas import tpu as pltpu
from jax.sharding import PartitionSpec as P

MESH = pl.DeviceIdType.MESH
F32 = jnp.float32
BF16 = jnp.bfloat16

NZ, NX, NY = 8, 4, 4
TOK = 128
D = 1024
FF = 512
TOPK = 8
HALF = D // 2
ROWS = NZ * TOK
BLOCK = 2 * TOK
NN = (((1,), (0,)), ((), ()))
NT = (((1,), (1,)), ((), ()))
TN = (((0,), (0,)), ((), ()))


def slot_of(offset):
    offset = offset % NZ
    if offset > NZ // 2:
        return 2 * (NZ - offset)
    return 2 * offset - 1 if offset else 0


def kernel(
    tok_in, up_in, w1_in, w2_in, ids, probs,
    mixed, igrad, sgrad, pgrad,
    tu, w1c, w2c, hid, hp, ps, part, rsb, rst,
    pts, ptr, pcs, pga, pgs, pgr,
    gown, gcs, gcr, gxa, gya, gyb, gxb, gs2,
    ag_s, ag_r, wx_s, wx_r, wy_s, wy_r, wc_s, wc_r, pt_s, pt_r, pg_s, pg_r,
    rs_s, rs_r, gc_s, gc_r, g1_s, g1_r, g2_s, g2_r, loc,
):
    section = lax.axis_index("section")
    y = lax.axis_index("dp")
    c = lax.axis_index("expert")
    z, x = section // NX, section % NX

    def at_z(j):
        return {"section": (z + j) % NZ * NX + x, "dp": y, "expert": c}

    def at_x(r):
        return {"section": z * NX + (x + r) % NX, "dp": y, "expert": c}

    def at_y(r):
        return {"section": section, "dp": (y + r) % NY, "expert": c}

    other_core = {"section": section, "dp": y, "expert": 1 - c}

    started = []

    def send(src, dst, s_sem, r_sem, device):
        copy = pltpu.make_async_remote_copy(
            src_ref=src, dst_ref=dst, send_sem=s_sem, recv_sem=r_sem,
            device_id=device, device_id_type=MESH,
        )
        copy.start()
        started.append(copy)

    def arrived(dst, s_sem, r_sem):
        pltpu.make_async_remote_copy(
            src_ref=dst, dst_ref=dst, send_sem=s_sem, recv_sem=r_sem,
            device_id=other_core, device_id_type=MESH,
        ).wait_recv()

    x_cols = pl.ds(pl.multiple_of(x * FF, FF), FF)
    local = [
        pltpu.make_async_copy(tok_in, tu.at[0, pl.ds(0, TOK)], loc.at[0]),
        pltpu.make_async_copy(up_in, tu.at[1, pl.ds(0, TOK)], loc.at[1]),
        pltpu.make_async_copy(w1_in.at[0], w1c.at[:, x_cols], loc.at[2]),
        pltpu.make_async_copy(w2_in.at[0], w2c.at[x_cols, :], loc.at[3]),
    ]
    for copy in local:
        copy.start()

    barrier = pltpu.get_barrier_semaphore()
    peers = [at_z(j) for j in range(1, NZ)] + [at_x(r) for r in range(1, NX)]
    peers += [at_y(r) for r in range(1, NY)] + [other_core]
    for peer in peers:
        pl.semaphore_signal(barrier, inc=1, device_id=peer, device_id_type=MESH)
    pl.semaphore_wait(barrier, len(peers))

    CH = TOK // 2
    sign = (1, -1)

    def ag_valid(h, d, a):
        return h <= 3 or (h == 4 and a == d)

    def ag_place(w, h, d, a):
        return tu.at[w, pl.ds(slot_of(-sign[d] * h) * TOK + a * CH, CH)]

    def ag_send(w, h, d, a):
        if h == 1:
            src = (tok_in, up_in)[w].at[pl.ds(a * CH, CH)]
        else:
            src = ag_place(w, h - 1, d, a)
        send(src, ag_place(w, h, d, a), ag_s.at[w, d, h - 1, a], ag_r.at[w, d, h - 1, a],
             at_z(sign[d]))

    def ag_hop(w, h, *chunks):
        for a in chunks or (0, 1):
            for d in range(2):
                if ag_valid(h, d, a):
                    arrived(ag_place(w, h, d, a), ag_s.at[w, d, h - 1, a], ag_r.at[w, d, h - 1, a])
                    if h < 4 and ag_valid(h + 1, d, a):
                        ag_send(w, h + 1, d, a)

    q_mine = (y % 2) * 2 + c
    q_next = ((y + 1) % 2) * 2 + c
    q_core = (y % 2) * 2 + 1 - c
    q_both = ((y + 1) % 2) * 2 + 1 - c

    def w_place(w, e, q, part_of=None):
        rows = D // 4 if w == 0 else FF // 4
        base, size = q * rows, rows
        if part_of is not None:
            size = rows // 2
            base = base + part_of * size
        if w == 0:
            return w1c.at[pl.ds(pl.multiple_of(base, size), size),
                          pl.ds(pl.multiple_of(e * FF, FF), FF)]
        return w2c.at[pl.ds(pl.multiple_of(e * FF + base, size), size), :]

    def wx_send(w, r):
        rows = D // 4 if w == 0 else FF // 4
        src = (w1_in, w2_in)[w].at[0, pl.ds(pl.multiple_of(q_mine * rows, rows), rows), :]
        send(src, w_place(w, x, q_mine), wx_s.at[w, r - 1], wx_r.at[w, 3 - r], at_x(r))

    def wx_relay(w, r):
        e = (x + r) % NX
        arrived(w_place(w, e, q_mine), wx_s.at[w, r - 1], wx_r.at[w, r - 1])
        for k, step in ((0, 1), (1, -1)):
            send(w_place(w, e, q_mine, k), w_place(w, e, q_mine, k),
                 wy_s.at[w, r - 1, k], wy_r.at[w, r - 1, k], at_y(step))
        send(w_place(w, e, q_mine), w_place(w, e, q_mine),
             wc_s.at[w, r - 1, 0], wc_r.at[w, r - 1, 0], other_core)

    def wy_relay(w, r):
        e = (x + r) % NX
        for k in range(2):
            arrived(w_place(w, e, q_next, k), wy_s.at[w, r - 1, k], wy_r.at[w, r - 1, k])
        send(w_place(w, e, q_next), w_place(w, e, q_next),
             wc_s.at[w, r - 1, 1], wc_r.at[w, r - 1, 1], other_core)

    def w_arrive(w, r):
        e = (x + r) % NX
        arrived(w_place(w, e, q_core), wc_s.at[w, r - 1, 0], wc_r.at[w, r - 1, 0])
        arrived(w_place(w, e, q_both), wc_s.at[w, r - 1, 1], wc_r.at[w, r - 1, 1])

    for w in range(2):
        for a in range(2):
            for d in range(2):
                ag_send(w, 1, d, a)
        for r in (1, 3, 2):
            wx_send(w, r)

    lane = lax.broadcasted_iota(jnp.int32, (TOK, TOK), 1)
    place = lax.broadcasted_iota(jnp.int32, (NZ * 8, TOK), 0)

    def place_of(k):
        e = ids[k:k + 1, :]
        return (e >> 2) * 8 + (e & 3)

    table = jnp.zeros((NZ * 8, TOK), F32)
    for k in range(TOPK):
        table += jnp.where(place == place_of(k), probs[k:k + 1, :], 0.0)
    pts[...] = table
    for j in range(1, NZ):
        there = slot_of(-j)
        send(pts.at[pl.ds(pl.multiple_of((z + j) % NZ * 8, 8), 8)], ptr.at[pl.ds(there * 8, 8)],
             pt_s.at[j - 1], pt_r.at[there - 1], at_z(j))
    ptr[0:8, :] = pts[pl.ds(pl.multiple_of(z * 8, 8), 8), :]
    pga[...] = jnp.zeros_like(pga)

    def columns(i):
        return pl.ds(pl.multiple_of(i * FF, FF), FF)

    def pre_block(first, size, e_from=0, e_to=NX):
        rows = pl.ds(first * TOK, size * TOK)

        def one(i, carry):
            pre = lax.dot_general(tu[0, rows, :], w1c[:, columns(i)], NN,
                                  preferred_element_type=F32)
            p = jnp.concatenate(
                [jnp.sum(jnp.where(lane == (first + k) * 8 + i, pcs[...], 0.0), axis=1,
                         keepdims=True) for k in range(size)], axis=0)
            sig = 0.5 * jnp.tanh(0.5 * pre) + 0.5
            act = pre * sig
            hid[rows, columns(i)] = act.astype(BF16)
            hp[rows, columns(i)] = (p * act).astype(BF16)
            ps[rows, columns(i)] = p * (sig * (1.0 + pre * (1.0 - sig)))
            return carry
        lax.fori_loop(e_from, e_to, one, 0)

    def mixed_block(first, size):
        rows = pl.ds(first * TOK, size * TOK)

        def one(n, carry):
            part[0, n, rows, :] = lax.dot_general(hp[rows, :], w2c[:, columns(n)], NN,
                                                  preferred_element_type=F32)
            return carry
        lax.fori_loop(0, 2, one, 0)

    def back_block(first, size, e_from=0, e_to=NX):
        rows = pl.ds(first * TOK, size * TOK)

        def one(i, carry):
            dhu = lax.dot_general(tu[1, rows, :], w2c[columns(i), :], NT,
                                  preferred_element_type=F32)
            col = jnp.sum(hid[rows, columns(i)].astype(F32) * dhu, axis=1, keepdims=True)
            total = pga[...]
            for k in range(size):
                total += jnp.where(lane == (first + k) * 8 + i, col[k * TOK:(k + 1) * TOK], 0.0)
            pga[...] = total
            hid[rows, columns(i)] = (dhu * ps[rows, columns(i)]).astype(BF16)
            return carry
        lax.fori_loop(e_from, e_to, one, 0)

    def input_block(first, size):
        rows = pl.ds(first * TOK, size * TOK)

        def one(n, carry):
            part[1, n, rows, :] = lax.dot_general(hid[rows, :], w1c[columns(n), :], NT,
                                                  preferred_element_type=F32)
            return carry
        lax.fori_loop(0, 2, one, 0)

    def weight_grad(hf):
        def one(i, carry):
            g = lax.dot_general(hp[:, columns(i)], tu[1, :, hf * HALF:(hf + 1) * HALF], TN,
                                preferred_element_type=F32).reshape(NY, 2, FF // 8, HALF)
            mine = c == 0
            gown[hf, i] = jnp.where(mine, g[:, 0], g[:, 1])
            gcs[hf, i] = jnp.where(mine, g[:, 1], g[:, 0]).astype(BF16)
            return carry
        lax.fori_loop(0, NX, one, 0)
        send(gcs.at[hf], gcr.at[hf], gc_s.at[hf], gc_r.at[hf], other_core)

    def rs_rows(d, j):
        return pl.ds(slot_of(sign[d] * j) * TOK, TOK)

    def rs_send(w, d, j, n, src):
        send(src, rsb.at[w, d, j - 1, n], rs_s.at[w, d, j - 1, n], rs_r.at[w, d, j - 1, n],
             at_z(sign[d]))

    def rs_arrived(w, d, j, n):
        arrived(rsb.at[w, d, j, n], rs_s.at[w, d, j, n], rs_r.at[w, d, j, n])

    def rs_start(w):
        for d in range(2):
            rst[w, d] = part[w, d, rs_rows(d, 4), :].astype(BF16)
            rs_send(w, d, 4, d, rst.at[w, d])
        for d in range(2):
            rsb[w, d, 3, 1 - d] = part[w, 1 - d, rs_rows(d, 3), :].astype(BF16)
            rs_send(w, d, 3, 1 - d, rsb.at[w, d, 3, 1 - d])

    def rs_step(w, j):
        for n in range(2):
            for d in range(2):
                half = 1 - d if n == 0 else d
                if j == 3 and n == 0:
                    continue
                rs_arrived(w, d, j, half)
                value = part[w, half, rs_rows(d, j), :] + rsb[w, d, j, half].astype(F32)
                rsb[w, d, j, half] = value.astype(BF16)
                rs_send(w, d, j, half, rsb.at[w, d, j, half])

    def rs_end(w, out):
        for n in range(2):
            value = part[w, n, pl.ds(0, TOK), :]
            for d in range(2):
                rs_arrived(w, d, 0, n)
                value = value + rsb[w, d, 0, n].astype(F32)
            out[:, n * HALF:(n + 1) * HALF] = value.astype(BF16)

    def grad_first(hf):
        arrived(gcr.at[hf], gc_s.at[hf], gc_r.at[hf])

        def one(i, carry):
            gcr[hf, i] = (gown[hf, i] + gcr[hf, i].astype(F32)).astype(BF16)
            return carry
        lax.fori_loop(0, NX, one, 0)
        for r in (1, 3, 2):
            if hf == 0:
                send(gcr.at[0, (x + r) % NX], gxa.at[3 - r],
                     g1_s.at[0, r - 1], g1_r.at[0, 3 - r], at_x(r))
            else:
                send(gcr.at[1, :, (y + r) % NY], gyb.at[3 - r],
                     g1_s.at[1, r - 1], g1_r.at[1, 3 - r], at_y(r))

    def grad_second(hf):
        total = gcr[0, x].astype(F32) if hf == 0 else gcr[1, :, y].astype(F32)
        landed = gxa if hf == 0 else gyb
        for k in range(3):
            arrived(landed.at[k], g1_s.at[hf, k], g1_r.at[hf, k])
            total = total + landed[k].astype(F32)
        gs2[hf] = total.astype(BF16)
        for r in (1, 3, 2):
            if hf == 0:
                send(gs2.at[0, (y + r) % NY], gya.at[3 - r],
                     g2_s.at[0, r - 1], g2_r.at[0, 3 - r], at_y(r))
            else:
                send(gs2.at[1, (x + r) % NX], gxb.at[3 - r],
                     g2_s.at[1, r - 1], g2_r.at[1, 3 - r], at_x(r))

    def grad_end(hf):
        total = gs2[0, y].astype(F32) if hf == 0 else gs2[1, x].astype(F32)
        landed = gya if hf == 0 else gxb
        for k in range(3):
            arrived(landed.at[k], g2_s.at[hf, k], g2_r.at[hf, k])
            total = total + landed[k].astype(F32)
        sgrad[0, :, hf * HALF:(hf + 1) * HALF] = total.astype(BF16)

    def p_columns():
        for k in range(1, NZ):
            arrived(ptr.at[pl.ds(k * 8, 8)], pt_s.at[k - 1], pt_r.at[k - 1])
        pcs[...] = jnp.concatenate([ptr[...], jnp.zeros((TOK - NZ * 8, TOK), F32)], axis=0).T

    def p_back():
        pgs[...] = pga[...].T[:NZ * 8]
        for j in range(1, NZ):
            send(pgs.at[pl.ds(slot_of(j) * 8, 8)], pgr.at[pl.ds(pl.multiple_of(z * 8, 8), 8)],
                 pg_s.at[j - 1], pg_r.at[NZ - 1 - j], at_z(j))
        pgr[pl.ds(pl.multiple_of(z * 8, 8), 8), :] = pgs[0:8, :]

    def p_end():
        for j in range(1, NZ):
            arrived(pgr.at[pl.ds(pl.multiple_of((z + j) % NZ * 8, 8), 8)],
                    pg_s.at[j - 1], pg_r.at[j - 1])
        for k in range(TOPK):
            pgrad[k:k + 1, :] = jnp.sum(jnp.where(place == place_of(k), pgr[...], 0.0), axis=0,
                                        keepdims=True)

    def each(f, w):
        for r in (1, 3, 2):
            f(w, r)

    ag_hop(0, 1)
    wx_relay(0, 1)
    wx_relay(0, 3)
    ag_hop(1, 1, 0)
    wx_relay(0, 2)
    ag_hop(1, 1, 1)
    p_columns()
    for copy in local:
        copy.wait()
    wy_relay(0, 1)
    wy_relay(0, 3)
    ag_hop(0, 2, 0)
    wy_relay(0, 2)
    ag_hop(0, 2, 1)
    each(wx_relay, 1)
    ag_hop(1, 2, 0)
    each(w_arrive, 0)
    pre_block(0, 4, 0, 2)
    ag_hop(1, 2, 1)
    pre_block(0, 4, 2, 4)
    each(wy_relay, 1)
    ag_hop(0, 3)
    pre_block(4, 3)
    ag_hop(1, 3, 0)
    each(w_arrive, 1)
    mixed_block(4, 3)
    ag_hop(1, 3, 1)
    back_block(0, 4, 0, 1)
    ag_hop(0, 4)
    pre_block(7, 1)
    mixed_block(7, 1)
    rs_start(0)
    back_block(4, 3)
    ag_hop(1, 4)
    back_block(7, 1)
    rs_step(0, 3)
    input_block(4, 4)
    rs_start(1)
    weight_grad(0)
    mixed_block(0, 4)
    rs_step(0, 2)
    grad_first(0)
    rs_step(1, 3)
    weight_grad(1)
    back_block(0, 4, 1, 3)
    rs_step(0, 1)
    grad_first(1)
    back_block(0, 4, 3, 4)
    input_block(0, 4)
    rs_step(1, 2)
    grad_second(0)
    p_back()
    early = len(started)
    rs_step(1, 1)
    grad_second(1)
    rs_end(0, mixed)
    p_end()
    grad_end(0)
    grad_end(1)
    for copy in started[:early]:
        copy.wait_send()
    rs_end(1, igrad)
    for copy in started[early:]:
        copy.wait_send()


def hand_over(a0, a1, a2, a3, b0, b1, b2, b3):
    for a, b in ((a0, b0), (a1, b1), (a2, b2), (a3, b3)):
        b[...] = a[...]


def body(tokens, expert_ids, probs, first_weight, second_weight, upstream):
    any_spec = pl.BlockSpec(memory_space=pl.ANY)
    vmem_spec = pl.BlockSpec(memory_space=pltpu.VMEM)
    dma = pltpu.SemaphoreType.DMA
    scratch = [
        pltpu.VMEM((2, ROWS, D), BF16),
        pltpu.VMEM((D, NX * FF), BF16),
        pltpu.VMEM((NX * FF, D), BF16),
        pltpu.VMEM((ROWS, NX * FF), BF16),
        pltpu.VMEM((ROWS, NX * FF), BF16),
        pltpu.VMEM((ROWS, NX * FF), F32),
        pltpu.VMEM((2, 2, ROWS, HALF), F32),
        pltpu.VMEM((2, 2, 4, 2, TOK, HALF), BF16),
        pltpu.VMEM((2, 2, TOK, HALF), BF16),
        pltpu.VMEM((NZ * 8, TOK), F32),
        pltpu.VMEM((NZ * 8, TOK), F32),
        pltpu.VMEM((TOK, TOK), F32),
        pltpu.VMEM((TOK, TOK), F32),
        pltpu.VMEM((NZ * 8, TOK), F32),
        pltpu.VMEM((NZ * 8, TOK), F32),
        pltpu.VMEM((2, NX, NY, FF // 8, HALF), F32),
        pltpu.VMEM((2, NX, NY, FF // 8, HALF), BF16),
        pltpu.VMEM((2, NX, NY, FF // 8, HALF), BF16),
        pltpu.VMEM((3, NY, FF // 8, HALF), BF16),
        pltpu.VMEM((3, FF // 8, HALF), BF16),
        pltpu.VMEM((3, NX, FF // 8, HALF), BF16),
        pltpu.VMEM((3, FF // 8, HALF), BF16),
        pltpu.VMEM((2, 4, FF // 8, HALF), BF16),
        dma((2, 2, 4, 2)), dma((2, 2, 4, 2)),
        dma((2, 3)), dma((2, 3)),
        dma((2, 3, 2)), dma((2, 3, 2)),
        dma((2, 3, 2)), dma((2, 3, 2)),
        dma((NZ - 1,)), dma((NZ - 1,)),
        dma((NZ - 1,)), dma((NZ - 1,)),
        dma((2, 2, 4, 2)), dma((2, 2, 4, 2)),
        dma((2,)), dma((2,)),
        dma((2, 3)), dma((2, 3)),
        dma((2, 3)), dma((2, 3)),
        dma((4,)),
    ]
    results = pl.pallas_call(
        kernel,
        out_shape=(
            jax.ShapeDtypeStruct((TOK, D), BF16),
            jax.ShapeDtypeStruct((TOK, D), BF16),
            jax.ShapeDtypeStruct((1, FF // 8, D), BF16),
            jax.ShapeDtypeStruct((TOPK, TOK), F32),
        ),
        in_specs=[any_spec] * 4 + [vmem_spec] * 2,
        out_specs=(vmem_spec,) * 4,
        scratch_shapes=scratch,
        compiler_params=pltpu.CompilerParams(
            collective_id=0, has_side_effects=True, vmem_limit_bytes=60 * 1024 * 1024
        ),
        cost_estimate=pl.CostEstimate(
            flops=2 * 5 * ROWS * D * NX * FF, bytes_accessed=8 * 1024 * 1024,
            transcendentals=ROWS * NX * FF,
        ),
    )(tokens, upstream, first_weight, second_weight, expert_ids.T, probs.T)
    mixed, igrad, sgrad, pgrad = pl.pallas_call(
        hand_over,
        out_shape=tuple(jax.ShapeDtypeStruct(r.shape, r.dtype) for r in results),
        in_specs=[vmem_spec] * 4,
        out_specs=(vmem_spec,) * 4,
    )(*results)
    return mixed, igrad, sgrad, pgrad.T


def solution(mesh):
    everything = P(("section", "dp", "expert"), None)
    return jax.shard_map(
        body,
        mesh=mesh,
        in_specs=(everything, everything, everything, P("section", None, None),
                  P("section", None, None), everything),
        out_specs=(everything, everything, P("section", ("dp", "expert"), None), everything),
        check_vma=False,
    )
```

```python
import jax
import jax.numpy as jnp
from jax import lax
from jax.experimental import pallas as pl
from jax.experimental.pallas import tpu as pltpu
from jax.sharding import PartitionSpec as P

MESH = pl.DeviceIdType.MESH
F32 = jnp.float32
BF16 = jnp.bfloat16

NZ, NX, NY = 8, 4, 4
TOK = 128
D = 1024
FF = 512
TOPK = 8
HALF = D // 2
ROWS = NZ * TOK
BLOCK = 2 * TOK
NN = (((1,), (0,)), ((), ()))
NT = (((1,), (1,)), ((), ()))
TN = (((0,), (0,)), ((), ()))


def slot_of(offset):
    offset = offset % NZ
    if offset > NZ // 2:
        return 2 * (NZ - offset)
    return 2 * offset - 1 if offset else 0


def kernel(
    tok_in, up_in, w1_in, w2_in, ids_in, probs_in,
    mixed_out, igrad_out, sgrad_out, pgrad_out,
    ids, probs, mixed, igrad, sgrad, pgrad,
    tu, w1c, w2c, hid, hp, ps, part, rsb, rst,
    pts, ptr, pcs, pga, pgs, pgr,
    gown, gcs, gcr, gxa, gya, gyb, gxb, gs2,
    ag_s, ag_r, wx_s, wx_r, wy_s, wy_r, wc_s, wc_r, pt_s, pt_r, pg_s, pg_r,
    rs_s, rs_r, gc_s, gc_r, g1_s, g1_r, g2_s, g2_r, loc,
):
    section = lax.axis_index("section")
    y = lax.axis_index("dp")
    c = lax.axis_index("expert")
    z, x = section // NX, section % NX

    def at_z(j):
        return {"section": (z + j) % NZ * NX + x, "dp": y, "expert": c}

    def at_x(r):
        return {"section": z * NX + (x + r) % NX, "dp": y, "expert": c}

    def at_y(r):
        return {"section": section, "dp": (y + r) % NY, "expert": c}

    other_core = {"section": section, "dp": y, "expert": 1 - c}

    started = []

    def send(src, dst, s_sem, r_sem, device):
        copy = pltpu.make_async_remote_copy(
            src_ref=src, dst_ref=dst, send_sem=s_sem, recv_sem=r_sem,
            device_id=device, device_id_type=MESH,
        )
        copy.start()
        started.append(copy)

    def arrived(dst, s_sem, r_sem):
        pltpu.make_async_remote_copy(
            src_ref=dst, dst_ref=dst, send_sem=s_sem, recv_sem=r_sem,
            device_id=other_core, device_id_type=MESH,
        ).wait_recv()

    x_cols = pl.ds(pl.multiple_of(x * FF, FF), FF)
    local = [
        pltpu.make_async_copy(tok_in, tu.at[0, pl.ds(0, TOK)], loc.at[0]),
        pltpu.make_async_copy(up_in, tu.at[1, pl.ds(0, TOK)], loc.at[1]),
        pltpu.make_async_copy(w1_in.at[0], w1c.at[:, x_cols], loc.at[2]),
        pltpu.make_async_copy(w2_in.at[0], w2c.at[x_cols, :], loc.at[3]),
    ]
    router = [
        pltpu.make_async_copy(ids_in, ids, loc.at[4]),
        pltpu.make_async_copy(probs_in, probs, loc.at[5]),
    ]
    for copy in router + local:
        copy.start()

    barrier = pltpu.get_barrier_semaphore()
    peers = [at_z(j) for j in range(1, NZ)] + [at_x(r) for r in range(1, NX)]
    peers += [at_y(r) for r in range(1, NY)] + [other_core]
    for peer in peers:
        pl.semaphore_signal(barrier, inc=1, device_id=peer, device_id_type=MESH)
    pl.semaphore_wait(barrier, len(peers))

    CH = TOK // 2
    sign = (1, -1)

    def ag_valid(h, d, a):
        return h <= 3 or (h == 4 and a == d)

    def ag_place(w, h, d, a):
        return tu.at[w, pl.ds(slot_of(-sign[d] * h) * TOK + a * CH, CH)]

    def ag_send(w, h, d, a):
        if h == 1:
            src = (tok_in, up_in)[w].at[pl.ds(a * CH, CH)]
        else:
            src = ag_place(w, h - 1, d, a)
        send(src, ag_place(w, h, d, a), ag_s.at[w, d, h - 1, a], ag_r.at[w, d, h - 1, a],
             at_z(sign[d]))

    def ag_hop(w, h, *chunks):
        for a in chunks or (0, 1):
            for d in range(2):
                if ag_valid(h, d, a):
                    arrived(ag_place(w, h, d, a), ag_s.at[w, d, h - 1, a], ag_r.at[w, d, h - 1, a])
                    if h < 4 and ag_valid(h + 1, d, a):
                        ag_send(w, h + 1, d, a)

    q_mine = (y % 2) * 2 + c
    q_next = ((y + 1) % 2) * 2 + c
    q_core = (y % 2) * 2 + 1 - c
    q_both = ((y + 1) % 2) * 2 + 1 - c

    def w_place(w, e, q, part_of=None):
        rows = D // 4 if w == 0 else FF // 4
        base, size = q * rows, rows
        if part_of is not None:
            size = rows // 2
            base = base + part_of * size
        if w == 0:
            return w1c.at[pl.ds(pl.multiple_of(base, size), size),
                          pl.ds(pl.multiple_of(e * FF, FF), FF)]
        return w2c.at[pl.ds(pl.multiple_of(e * FF + base, size), size), :]

    def wx_send(w, r):
        rows = D // 4 if w == 0 else FF // 4
        src = (w1_in, w2_in)[w].at[0, pl.ds(pl.multiple_of(q_mine * rows, rows), rows), :]
        send(src, w_place(w, x, q_mine), wx_s.at[w, r - 1], wx_r.at[w, 3 - r], at_x(r))

    def wx_relay(w, r):
        e = (x + r) % NX
        arrived(w_place(w, e, q_mine), wx_s.at[w, r - 1], wx_r.at[w, r - 1])
        for k, step in ((0, 1), (1, -1)):
            send(w_place(w, e, q_mine, k), w_place(w, e, q_mine, k),
                 wy_s.at[w, r - 1, k], wy_r.at[w, r - 1, k], at_y(step))
        send(w_place(w, e, q_mine), w_place(w, e, q_mine),
             wc_s.at[w, r - 1, 0], wc_r.at[w, r - 1, 0], other_core)

    def wy_relay(w, r):
        e = (x + r) % NX
        for k in range(2):
            arrived(w_place(w, e, q_next, k), wy_s.at[w, r - 1, k], wy_r.at[w, r - 1, k])
        send(w_place(w, e, q_next), w_place(w, e, q_next),
             wc_s.at[w, r - 1, 1], wc_r.at[w, r - 1, 1], other_core)

    def w_arrive(w, r):
        e = (x + r) % NX
        arrived(w_place(w, e, q_core), wc_s.at[w, r - 1, 0], wc_r.at[w, r - 1, 0])
        arrived(w_place(w, e, q_both), wc_s.at[w, r - 1, 1], wc_r.at[w, r - 1, 1])

    for w in range(2):
        for a in range(2):
            for d in range(2):
                ag_send(w, 1, d, a)
        for r in (1, 3, 2):
            wx_send(w, r)

    lane = lax.broadcasted_iota(jnp.int32, (TOK, TOK), 1)
    place = lax.broadcasted_iota(jnp.int32, (NZ * 8, TOK), 0)

    for copy in router:
        copy.wait()

    def place_of(k):
        e = ids[k:k + 1, :]
        return (e >> 2) * 8 + (e & 3)

    table = jnp.zeros((NZ * 8, TOK), F32)
    for k in range(TOPK):
        table += jnp.where(place == place_of(k), probs[k:k + 1, :], 0.0)
    pts[...] = table
    for j in range(1, NZ):
        there = slot_of(-j)
        send(pts.at[pl.ds(pl.multiple_of((z + j) % NZ * 8, 8), 8)], ptr.at[pl.ds(there * 8, 8)],
             pt_s.at[j - 1], pt_r.at[there - 1], at_z(j))
    ptr[0:8, :] = pts[pl.ds(pl.multiple_of(z * 8, 8), 8), :]
    pga[...] = jnp.zeros_like(pga)

    def columns(i):
        return pl.ds(pl.multiple_of(i * FF, FF), FF)

    def pre_block(first, size, e_from=0, e_to=NX):
        rows = pl.ds(first * TOK, size * TOK)

        def one(i, carry):
            pre = lax.dot_general(tu[0, rows, :], w1c[:, columns(i)], NN,
                                  preferred_element_type=F32)
            p = jnp.concatenate(
                [jnp.sum(jnp.where(lane == (first + k) * 8 + i, pcs[...], 0.0), axis=1,
                         keepdims=True) for k in range(size)], axis=0)
            sig = 0.5 * jnp.tanh(0.5 * pre) + 0.5
            act = pre * sig
            hid[rows, columns(i)] = act.astype(BF16)
            hp[rows, columns(i)] = (p * act).astype(BF16)
            ps[rows, columns(i)] = p * (sig * (1.0 + pre * (1.0 - sig)))
            return carry
        lax.fori_loop(e_from, e_to, one, 0)

    def mixed_block(first, size):
        rows = pl.ds(first * TOK, size * TOK)

        def one(n, carry):
            part[0, n, rows, :] = lax.dot_general(hp[rows, :], w2c[:, columns(n)], NN,
                                                  preferred_element_type=F32)
            return carry
        lax.fori_loop(0, 2, one, 0)

    def back_block(first, size, e_from=0, e_to=NX):
        rows = pl.ds(first * TOK, size * TOK)

        def one(i, carry):
            dhu = lax.dot_general(tu[1, rows, :], w2c[columns(i), :], NT,
                                  preferred_element_type=F32)
            col = jnp.sum(hid[rows, columns(i)].astype(F32) * dhu, axis=1, keepdims=True)
            total = pga[...]
            for k in range(size):
                total += jnp.where(lane == (first + k) * 8 + i, col[k * TOK:(k + 1) * TOK], 0.0)
            pga[...] = total
            hid[rows, columns(i)] = (dhu * ps[rows, columns(i)]).astype(BF16)
            return carry
        lax.fori_loop(e_from, e_to, one, 0)

    def input_block(first, size):
        rows = pl.ds(first * TOK, size * TOK)

        def one(n, carry):
            part[1, n, rows, :] = lax.dot_general(hid[rows, :], w1c[columns(n), :], NT,
                                                  preferred_element_type=F32)
            return carry
        lax.fori_loop(0, 2, one, 0)

    def weight_grad(hf):
        def one(i, carry):
            g = lax.dot_general(hp[:, columns(i)], tu[1, :, hf * HALF:(hf + 1) * HALF], TN,
                                preferred_element_type=F32).reshape(NY, 2, FF // 8, HALF)
            mine = c == 0
            gown[hf, i] = jnp.where(mine, g[:, 0], g[:, 1])
            gcs[hf, i] = jnp.where(mine, g[:, 1], g[:, 0]).astype(BF16)
            return carry
        lax.fori_loop(0, NX, one, 0)
        send(gcs.at[hf], gcr.at[hf], gc_s.at[hf], gc_r.at[hf], other_core)

    def rs_rows(d, j):
        return pl.ds(slot_of(sign[d] * j) * TOK, TOK)

    def rs_send(w, d, j, n, src):
        send(src, rsb.at[w, d, j - 1, n], rs_s.at[w, d, j - 1, n], rs_r.at[w, d, j - 1, n],
             at_z(sign[d]))

    def rs_arrived(w, d, j, n):
        arrived(rsb.at[w, d, j, n], rs_s.at[w, d, j, n], rs_r.at[w, d, j, n])

    def rs_start(w):
        for d in range(2):
            rst[w, d] = part[w, d, rs_rows(d, 4), :].astype(BF16)
            rs_send(w, d, 4, d, rst.at[w, d])
        for d in range(2):
            rsb[w, d, 3, 1 - d] = part[w, 1 - d, rs_rows(d, 3), :].astype(BF16)
            rs_send(w, d, 3, 1 - d, rsb.at[w, d, 3, 1 - d])

    def rs_step(w, j):
        for n in range(2):
            for d in range(2):
                half = 1 - d if n == 0 else d
                if j == 3 and n == 0:
                    continue
                rs_arrived(w, d, j, half)
                value = part[w, half, rs_rows(d, j), :] + rsb[w, d, j, half].astype(F32)
                rsb[w, d, j, half] = value.astype(BF16)
                rs_send(w, d, j, half, rsb.at[w, d, j, half])

    def rs_end(w, out):
        for n in range(2):
            value = part[w, n, pl.ds(0, TOK), :]
            for d in range(2):
                rs_arrived(w, d, 0, n)
                value = value + rsb[w, d, 0, n].astype(F32)
            out[:, n * HALF:(n + 1) * HALF] = value.astype(BF16)

    def grad_first(hf):
        arrived(gcr.at[hf], gc_s.at[hf], gc_r.at[hf])

        def one(i, carry):
            gcr[hf, i] = (gown[hf, i] + gcr[hf, i].astype(F32)).astype(BF16)
            return carry
        lax.fori_loop(0, NX, one, 0)
        for r in (1, 3, 2):
            if hf == 0:
                send(gcr.at[0, (x + r) % NX], gxa.at[3 - r],
                     g1_s.at[0, r - 1], g1_r.at[0, 3 - r], at_x(r))
            else:
                send(gcr.at[1, :, (y + r) % NY], gyb.at[3 - r],
                     g1_s.at[1, r - 1], g1_r.at[1, 3 - r], at_y(r))

    def grad_second(hf):
        total = gcr[0, x].astype(F32) if hf == 0 else gcr[1, :, y].astype(F32)
        landed = gxa if hf == 0 else gyb
        for k in range(3):
            arrived(landed.at[k], g1_s.at[hf, k], g1_r.at[hf, k])
            total = total + landed[k].astype(F32)
        gs2[hf] = total.astype(BF16)
        for r in (1, 3, 2):
            if hf == 0:
                send(gs2.at[0, (y + r) % NY], gya.at[3 - r],
                     g2_s.at[0, r - 1], g2_r.at[0, 3 - r], at_y(r))
            else:
                send(gs2.at[1, (x + r) % NX], gxb.at[3 - r],
                     g2_s.at[1, r - 1], g2_r.at[1, 3 - r], at_x(r))

    def grad_end(hf):
        total = gs2[0, y].astype(F32) if hf == 0 else gs2[1, x].astype(F32)
        landed = gya if hf == 0 else gxb
        for k in range(3):
            arrived(landed.at[k], g2_s.at[hf, k], g2_r.at[hf, k])
            total = total + landed[k].astype(F32)
        sgrad[0, :, hf * HALF:(hf + 1) * HALF] = total.astype(BF16)

    def p_columns():
        for k in range(1, NZ):
            arrived(ptr.at[pl.ds(k * 8, 8)], pt_s.at[k - 1], pt_r.at[k - 1])
        pcs[...] = jnp.concatenate([ptr[...], jnp.zeros((TOK - NZ * 8, TOK), F32)], axis=0).T

    def p_back():
        pgs[...] = pga[...].T[:NZ * 8]
        for j in range(1, NZ):
            send(pgs.at[pl.ds(slot_of(j) * 8, 8)], pgr.at[pl.ds(pl.multiple_of(z * 8, 8), 8)],
                 pg_s.at[j - 1], pg_r.at[NZ - 1 - j], at_z(j))
        pgr[pl.ds(pl.multiple_of(z * 8, 8), 8), :] = pgs[0:8, :]

    def p_end():
        for j in range(1, NZ):
            arrived(pgr.at[pl.ds(pl.multiple_of((z + j) % NZ * 8, 8), 8)],
                    pg_s.at[j - 1], pg_r.at[j - 1])
        for k in range(TOPK):
            pgrad[k:k + 1, :] = jnp.sum(jnp.where(place == place_of(k), pgr[...], 0.0), axis=0,
                                        keepdims=True)

    def each(f, w):
        for r in (1, 3, 2):
            f(w, r)

    ag_hop(0, 1)
    wx_relay(0, 1)
    wx_relay(0, 3)
    ag_hop(1, 1, 0)
    wx_relay(0, 2)
    ag_hop(1, 1, 1)
    p_columns()
    for copy in local:
        copy.wait()
    wy_relay(0, 1)
    wy_relay(0, 3)
    ag_hop(0, 2, 0)
    wy_relay(0, 2)
    ag_hop(0, 2, 1)
    each(wx_relay, 1)
    ag_hop(1, 2, 0)
    each(w_arrive, 0)
    pre_block(0, 4, 0, 2)
    ag_hop(1, 2, 1)
    pre_block(0, 4, 2, 4)
    each(wy_relay, 1)
    ag_hop(0, 3)
    pre_block(4, 3)
    ag_hop(1, 3, 0)
    each(w_arrive, 1)
    mixed_block(4, 3)
    ag_hop(1, 3, 1)
    back_block(0, 4, 0, 1)
    ag_hop(0, 4)
    pre_block(7, 1)
    mixed_block(7, 1)
    rs_start(0)
    back_block(4, 3)
    ag_hop(1, 4)
    back_block(7, 1)
    rs_step(0, 3)
    input_block(4, 4)
    rs_start(1)
    weight_grad(0)
    mixed_block(0, 4)
    rs_step(0, 2)
    grad_first(0)
    rs_step(1, 3)
    weight_grad(1)
    back_block(0, 4, 1, 3)
    rs_step(0, 1)
    grad_first(1)
    back_block(0, 4, 3, 4)
    input_block(0, 4)
    rs_step(1, 2)
    grad_second(0)
    p_back()
    early = len(started)
    rs_step(1, 1)
    grad_second(1)
    rs_end(0, mixed)
    p_end()
    results = [
        pltpu.make_async_copy(mixed, mixed_out, loc.at[6]),
        pltpu.make_async_copy(pgrad, pgrad_out, loc.at[7]),
        pltpu.make_async_copy(sgrad, sgrad_out, loc.at[8]),
        pltpu.make_async_copy(igrad, igrad_out, loc.at[9]),
    ]
    results[0].start()
    results[1].start()
    grad_end(0)
    grad_end(1)
    results[2].start()
    for copy in started[:early]:
        copy.wait_send()
    rs_end(1, igrad)
    results[3].start()
    for copy in results:
        copy.wait()
    for copy in started[early:]:
        copy.wait_send()


def hand_over(a0, a1, a2, a3, b0, b1, b2, b3):
    for a, b in ((a0, b0), (a1, b1), (a2, b2), (a3, b3)):
        b[...] = a[...]


def body(tokens, expert_ids, probs, first_weight, second_weight, upstream):
    any_spec = pl.BlockSpec(memory_space=pl.ANY)
    vmem_spec = pl.BlockSpec(memory_space=pltpu.VMEM)
    dma = pltpu.SemaphoreType.DMA
    scratch = [
        pltpu.VMEM((TOPK, TOK), jnp.int32),
        pltpu.VMEM((TOPK, TOK), F32),
        pltpu.VMEM((TOK, D), BF16),
        pltpu.VMEM((TOK, D), BF16),
        pltpu.VMEM((1, FF // 8, D), BF16),
        pltpu.VMEM((TOPK, TOK), F32),
        pltpu.VMEM((2, ROWS, D), BF16),
        pltpu.VMEM((D, NX * FF), BF16),
        pltpu.VMEM((NX * FF, D), BF16),
        pltpu.VMEM((ROWS, NX * FF), BF16),
        pltpu.VMEM((ROWS, NX * FF), BF16),
        pltpu.VMEM((ROWS, NX * FF), F32),
        pltpu.VMEM((2, 2, ROWS, HALF), F32),
        pltpu.VMEM((2, 2, 4, 2, TOK, HALF), BF16),
        pltpu.VMEM((2, 2, TOK, HALF), BF16),
        pltpu.VMEM((NZ * 8, TOK), F32),
        pltpu.VMEM((NZ * 8, TOK), F32),
        pltpu.VMEM((TOK, TOK), F32),
        pltpu.VMEM((TOK, TOK), F32),
        pltpu.VMEM((NZ * 8, TOK), F32),
        pltpu.VMEM((NZ * 8, TOK), F32),
        pltpu.VMEM((2, NX, NY, FF // 8, HALF), F32),
        pltpu.VMEM((2, NX, NY, FF // 8, HALF), BF16),
        pltpu.VMEM((2, NX, NY, FF // 8, HALF), BF16),
        pltpu.VMEM((3, NY, FF // 8, HALF), BF16),
        pltpu.VMEM((3, FF // 8, HALF), BF16),
        pltpu.VMEM((3, NX, FF // 8, HALF), BF16),
        pltpu.VMEM((3, FF // 8, HALF), BF16),
        pltpu.VMEM((2, 4, FF // 8, HALF), BF16),
        dma((2, 2, 4, 2)), dma((2, 2, 4, 2)),
        dma((2, 3)), dma((2, 3)),
        dma((2, 3, 2)), dma((2, 3, 2)),
        dma((2, 3, 2)), dma((2, 3, 2)),
        dma((NZ - 1,)), dma((NZ - 1,)),
        dma((NZ - 1,)), dma((NZ - 1,)),
        dma((2, 2, 4, 2)), dma((2, 2, 4, 2)),
        dma((2,)), dma((2,)),
        dma((2, 3)), dma((2, 3)),
        dma((2, 3)), dma((2, 3)),
        dma((10,)),
    ]
    results = pl.pallas_call(
        kernel,
        out_shape=(
            jax.ShapeDtypeStruct((TOK, D), BF16),
            jax.ShapeDtypeStruct((TOK, D), BF16),
            jax.ShapeDtypeStruct((1, FF // 8, D), BF16),
            jax.ShapeDtypeStruct((TOPK, TOK), F32),
        ),
        in_specs=[any_spec] * 6,
        out_specs=(any_spec,) * 4,
        scratch_shapes=scratch,
        compiler_params=pltpu.CompilerParams(
            collective_id=0, has_side_effects=True, vmem_limit_bytes=60 * 1024 * 1024
        ),
        cost_estimate=pl.CostEstimate(
            flops=2 * 5 * ROWS * D * NX * FF, bytes_accessed=8 * 1024 * 1024,
            transcendentals=ROWS * NX * FF,
        ),
    )(tokens, upstream, first_weight, second_weight, expert_ids.T, probs.T)
    mixed, igrad, sgrad, pgrad = pl.pallas_call(
        hand_over,
        out_shape=tuple(jax.ShapeDtypeStruct(r.shape, r.dtype) for r in results),
        in_specs=[vmem_spec] * 4,
        out_specs=(vmem_spec,) * 4,
    )(*results)
    return mixed, igrad, sgrad, pgrad.T


def solution(mesh):
    everything = P(("section", "dp", "expert"), None)
    return jax.shard_map(
        body,
        mesh=mesh,
        in_specs=(everything, everything, everything, P("section", None, None),
                  P("section", None, None), everything),
        out_specs=(everything, everything, P("section", ("dp", "expert"), None), everything),
        check_vma=False,
    )
```

```python
import jax
import jax.numpy as jnp
from jax import lax
from jax.experimental import pallas as pl
from jax.experimental.pallas import tpu as pltpu
from jax.sharding import PartitionSpec as P

MESH = pl.DeviceIdType.MESH
F32 = jnp.float32
BF16 = jnp.bfloat16

NZ, NX, NY = 8, 4, 4
TOK = 128
D = 1024
FF = 512
TOPK = 8
HALF = D // 2
ROWS = NZ * TOK
BLOCK = 2 * TOK
NN = (((1,), (0,)), ((), ()))
NT = (((1,), (1,)), ((), ()))
TN = (((0,), (0,)), ((), ()))


def slot_of(offset):
    offset = offset % NZ
    if offset > NZ // 2:
        return 2 * (NZ - offset)
    return 2 * offset - 1 if offset else 0


def kernel(
    tok_in, up_in, w1_in, w2_in, ids_in, probs_in,
    mixed_out, igrad_out, sgrad_out, pgrad_out,
    ids, probs, mixed, igrad, sgrad, pgrad,
    tu, w1c, w2c, hid, hp, ps, part, rsb, rst,
    pts, ptr, pcs, pga, pgs, pgr,
    gown, gcs, gcr, gxa, gya, gyb, gxb, gs2,
    ag_s, ag_r, wx_s, wx_r, wy_s, wy_r, wc_s, wc_r, pt_s, pt_r, pg_s, pg_r,
    rs_s, rs_r, gc_s, gc_r, g1_s, g1_r, g2_s, g2_r, loc,
):
    section = lax.axis_index("section")
    y = lax.axis_index("dp")
    c = lax.axis_index("expert")
    z, x = section // NX, section % NX

    def at_z(j):
        return {"section": (z + j) % NZ * NX + x, "dp": y, "expert": c}

    def at_x(r):
        return {"section": z * NX + (x + r) % NX, "dp": y, "expert": c}

    def at_y(r):
        return {"section": section, "dp": (y + r) % NY, "expert": c}

    other_core = {"section": section, "dp": y, "expert": 1 - c}

    started = []

    def send(src, dst, s_sem, r_sem, device):
        copy = pltpu.make_async_remote_copy(
            src_ref=src, dst_ref=dst, send_sem=s_sem, recv_sem=r_sem,
            device_id=device, device_id_type=MESH,
        )
        copy.start()
        started.append(copy)

    def arrived(dst, s_sem, r_sem):
        pltpu.make_async_remote_copy(
            src_ref=dst, dst_ref=dst, send_sem=s_sem, recv_sem=r_sem,
            device_id=other_core, device_id_type=MESH,
        ).wait_recv()

    x_cols = pl.ds(pl.multiple_of(x * FF, FF), FF)
    local = [
        pltpu.make_async_copy(tok_in, tu.at[0, pl.ds(0, TOK)], loc.at[0]),
        pltpu.make_async_copy(up_in, tu.at[1, pl.ds(0, TOK)], loc.at[1]),
        pltpu.make_async_copy(w1_in.at[0], w1c.at[:, x_cols], loc.at[2]),
        pltpu.make_async_copy(w2_in.at[0], w2c.at[x_cols, :], loc.at[3]),
    ]
    router = [
        pltpu.make_async_copy(ids_in, ids, loc.at[4]),
        pltpu.make_async_copy(probs_in, probs, loc.at[5]),
    ]
    for copy in router + local:
        copy.start()

    barrier = pltpu.get_barrier_semaphore()
    peers = [at_z(j) for j in range(1, NZ)] + [at_x(r) for r in range(1, NX)]
    peers += [at_y(r) for r in range(1, NY)] + [other_core]
    for peer in peers:
        pl.semaphore_signal(barrier, inc=1, device_id=peer, device_id_type=MESH)
    pl.semaphore_wait(barrier, len(peers))

    CH = TOK // 2
    sign = (1, -1)

    def ag_valid(h, d, a):
        return h <= 3 or (h == 4 and a == d)

    def ag_place(w, h, d, a):
        return tu.at[w, pl.ds(slot_of(-sign[d] * h) * TOK + a * CH, CH)]

    def ag_send(w, h, d, a):
        if h == 1:
            src = (tok_in, up_in)[w].at[pl.ds(a * CH, CH)]
        else:
            src = ag_place(w, h - 1, d, a)
        send(src, ag_place(w, h, d, a), ag_s.at[w, d, h - 1, a], ag_r.at[w, d, h - 1, a],
             at_z(sign[d]))

    def ag_hop(w, h, *chunks):
        for a in chunks or (0, 1):
            for d in range(2):
                if ag_valid(h, d, a):
                    arrived(ag_place(w, h, d, a), ag_s.at[w, d, h - 1, a], ag_r.at[w, d, h - 1, a])
                    if h < 4 and ag_valid(h + 1, d, a):
                        ag_send(w, h + 1, d, a)

    q_mine = (y % 2) * 2 + c
    q_next = ((y + 1) % 2) * 2 + c
    q_core = (y % 2) * 2 + 1 - c
    q_both = ((y + 1) % 2) * 2 + 1 - c

    def w_place(w, e, q, part_of=None):
        rows = D // 4 if w == 0 else FF // 4
        base, size = q * rows, rows
        if part_of is not None:
            size = rows // 2
            base = base + part_of * size
        if w == 0:
            return w1c.at[pl.ds(pl.multiple_of(base, size), size),
                          pl.ds(pl.multiple_of(e * FF, FF), FF)]
        return w2c.at[pl.ds(pl.multiple_of(e * FF + base, size), size), :]

    def wx_send(w, r):
        rows = D // 4 if w == 0 else FF // 4
        src = (w1_in, w2_in)[w].at[0, pl.ds(pl.multiple_of(q_mine * rows, rows), rows), :]
        send(src, w_place(w, x, q_mine), wx_s.at[w, r - 1], wx_r.at[w, 3 - r], at_x(r))

    def wx_relay(w, r):
        e = (x + r) % NX
        arrived(w_place(w, e, q_mine), wx_s.at[w, r - 1], wx_r.at[w, r - 1])
        for k, step in ((0, 1), (1, -1)):
            send(w_place(w, e, q_mine, k), w_place(w, e, q_mine, k),
                 wy_s.at[w, r - 1, k], wy_r.at[w, r - 1, k], at_y(step))
        send(w_place(w, e, q_mine), w_place(w, e, q_mine),
             wc_s.at[w, r - 1, 0], wc_r.at[w, r - 1, 0], other_core)

    def wy_relay(w, r):
        e = (x + r) % NX
        for k in range(2):
            arrived(w_place(w, e, q_next, k), wy_s.at[w, r - 1, k], wy_r.at[w, r - 1, k])
        send(w_place(w, e, q_next), w_place(w, e, q_next),
             wc_s.at[w, r - 1, 1], wc_r.at[w, r - 1, 1], other_core)

    def w_arrive(w, r):
        e = (x + r) % NX
        arrived(w_place(w, e, q_core), wc_s.at[w, r - 1, 0], wc_r.at[w, r - 1, 0])
        arrived(w_place(w, e, q_both), wc_s.at[w, r - 1, 1], wc_r.at[w, r - 1, 1])

    for w in range(2):
        for a in range(2):
            for d in range(2):
                ag_send(w, 1, d, a)
        for r in (1, 3, 2):
            wx_send(w, r)

    lane = lax.broadcasted_iota(jnp.int32, (TOK, TOK), 1)
    place = lax.broadcasted_iota(jnp.int32, (NZ * 8, TOK), 0)

    for copy in router:
        copy.wait()

    def place_of(k):
        e = ids[k:k + 1, :]
        return (e >> 2) * 8 + (e & 3)

    table = jnp.zeros((NZ * 8, TOK), F32)
    for k in range(TOPK):
        table += jnp.where(place == place_of(k), probs[k:k + 1, :], 0.0)
    pts[...] = table
    for j in range(1, NZ):
        there = slot_of(-j)
        send(pts.at[pl.ds(pl.multiple_of((z + j) % NZ * 8, 8), 8)], ptr.at[pl.ds(there * 8, 8)],
             pt_s.at[j - 1], pt_r.at[there - 1], at_z(j))
    ptr[0:8, :] = pts[pl.ds(pl.multiple_of(z * 8, 8), 8), :]
    pga[...] = jnp.zeros_like(pga)

    def columns(i):
        return pl.ds(pl.multiple_of(i * FF, FF), FF)

    def pre_block(first, size, e_from=0, e_to=NX):
        rows = pl.ds(first * TOK, size * TOK)

        def one(i, carry):
            pre = lax.dot_general(tu[0, rows, :], w1c[:, columns(i)], NN,
                                  preferred_element_type=F32)
            p = jnp.concatenate(
                [jnp.sum(jnp.where(lane == (first + k) * 8 + i, pcs[...], 0.0), axis=1,
                         keepdims=True) for k in range(size)], axis=0)
            sig = 0.5 * jnp.tanh(0.5 * pre) + 0.5
            act = pre * sig
            hid[rows, columns(i)] = act.astype(BF16)
            hp[rows, columns(i)] = (p * act).astype(BF16)
            ps[rows, columns(i)] = p * (sig * (1.0 + pre * (1.0 - sig)))
            return carry
        lax.fori_loop(e_from, e_to, one, 0)

    def mixed_block(first, size):
        rows = pl.ds(first * TOK, size * TOK)

        def one(n, carry):
            part[0, n, rows, :] = lax.dot_general(hp[rows, :], w2c[:, columns(n)], NN,
                                                  preferred_element_type=F32)
            return carry
        lax.fori_loop(0, 2, one, 0)

    def back_block(first, size, e_from=0, e_to=NX):
        rows = pl.ds(first * TOK, size * TOK)

        def one(i, carry):
            dhu = lax.dot_general(tu[1, rows, :], w2c[columns(i), :], NT,
                                  preferred_element_type=F32)
            col = jnp.sum(hid[rows, columns(i)].astype(F32) * dhu, axis=1, keepdims=True)
            total = pga[...]
            for k in range(size):
                total += jnp.where(lane == (first + k) * 8 + i, col[k * TOK:(k + 1) * TOK], 0.0)
            pga[...] = total
            hid[rows, columns(i)] = (dhu * ps[rows, columns(i)]).astype(BF16)
            return carry
        lax.fori_loop(e_from, e_to, one, 0)

    def input_block(first, size):
        rows = pl.ds(first * TOK, size * TOK)

        def one(n, carry):
            part[1, n, rows, :] = lax.dot_general(hid[rows, :], w1c[columns(n), :], NT,
                                                  preferred_element_type=F32)
            return carry
        lax.fori_loop(0, 2, one, 0)

    def weight_grad(hf):
        def one(i, carry):
            g = lax.dot_general(hp[:, columns(i)], tu[1, :, hf * HALF:(hf + 1) * HALF], TN,
                                preferred_element_type=F32).reshape(NY, 2, FF // 8, HALF)
            mine = c == 0
            gown[hf, i] = jnp.where(mine, g[:, 0], g[:, 1])
            gcs[hf, i] = jnp.where(mine, g[:, 1], g[:, 0]).astype(BF16)
            return carry
        lax.fori_loop(0, NX, one, 0)
        send(gcs.at[hf], gcr.at[hf], gc_s.at[hf], gc_r.at[hf], other_core)

    def rs_rows(d, j):
        return pl.ds(slot_of(sign[d] * j) * TOK, TOK)

    def rs_send(w, d, j, n, src):
        send(src, rsb.at[w, d, j - 1, n], rs_s.at[w, d, j - 1, n], rs_r.at[w, d, j - 1, n],
             at_z(sign[d]))

    def rs_arrived(w, d, j, n):
        arrived(rsb.at[w, d, j, n], rs_s.at[w, d, j, n], rs_r.at[w, d, j, n])

    def rs_start(w):
        for d in range(2):
            rst[w, d] = part[w, d, rs_rows(d, 4), :].astype(BF16)
            rs_send(w, d, 4, d, rst.at[w, d])
        for d in range(2):
            rsb[w, d, 3, 1 - d] = part[w, 1 - d, rs_rows(d, 3), :].astype(BF16)
            rs_send(w, d, 3, 1 - d, rsb.at[w, d, 3, 1 - d])

    def rs_step(w, j):
        for n in range(2):
            for d in range(2):
                half = 1 - d if n == 0 else d
                if j == 3 and n == 0:
                    continue
                rs_arrived(w, d, j, half)
                value = part[w, half, rs_rows(d, j), :] + rsb[w, d, j, half].astype(F32)
                rsb[w, d, j, half] = value.astype(BF16)
                rs_send(w, d, j, half, rsb.at[w, d, j, half])

    def rs_end(w, out):
        for n in range(2):
            value = part[w, n, pl.ds(0, TOK), :]
            for d in range(2):
                rs_arrived(w, d, 0, n)
                value = value + rsb[w, d, 0, n].astype(F32)
            out[:, n * HALF:(n + 1) * HALF] = value.astype(BF16)

    def grad_first(hf):
        arrived(gcr.at[hf], gc_s.at[hf], gc_r.at[hf])

        def one(i, carry):
            gcr[hf, i] = (gown[hf, i] + gcr[hf, i].astype(F32)).astype(BF16)
            return carry
        lax.fori_loop(0, NX, one, 0)
        for r in (1, 3, 2):
            if hf == 0:
                send(gcr.at[0, (x + r) % NX], gxa.at[3 - r],
                     g1_s.at[0, r - 1], g1_r.at[0, 3 - r], at_x(r))
            else:
                send(gcr.at[1, :, (y + r) % NY], gyb.at[3 - r],
                     g1_s.at[1, r - 1], g1_r.at[1, 3 - r], at_y(r))

    def grad_second(hf):
        total = gcr[0, x].astype(F32) if hf == 0 else gcr[1, :, y].astype(F32)
        landed = gxa if hf == 0 else gyb
        for k in range(3):
            arrived(landed.at[k], g1_s.at[hf, k], g1_r.at[hf, k])
            total = total + landed[k].astype(F32)
        gs2[hf] = total.astype(BF16)
        for r in (1, 3, 2):
            if hf == 0:
                send(gs2.at[0, (y + r) % NY], gya.at[3 - r],
                     g2_s.at[0, r - 1], g2_r.at[0, 3 - r], at_y(r))
            else:
                send(gs2.at[1, (x + r) % NX], gxb.at[3 - r],
                     g2_s.at[1, r - 1], g2_r.at[1, 3 - r], at_x(r))

    def grad_end(hf):
        total = gs2[0, y].astype(F32) if hf == 0 else gs2[1, x].astype(F32)
        landed = gya if hf == 0 else gxb
        for k in range(3):
            arrived(landed.at[k], g2_s.at[hf, k], g2_r.at[hf, k])
            total = total + landed[k].astype(F32)
        sgrad[0, :, hf * HALF:(hf + 1) * HALF] = total.astype(BF16)

    def p_columns():
        for k in range(1, NZ):
            arrived(ptr.at[pl.ds(k * 8, 8)], pt_s.at[k - 1], pt_r.at[k - 1])
        pcs[...] = jnp.concatenate([ptr[...], jnp.zeros((TOK - NZ * 8, TOK), F32)], axis=0).T

    def p_back():
        pgs[...] = pga[...].T[:NZ * 8]
        for j in range(1, NZ):
            send(pgs.at[pl.ds(slot_of(j) * 8, 8)], pgr.at[pl.ds(pl.multiple_of(z * 8, 8), 8)],
                 pg_s.at[j - 1], pg_r.at[NZ - 1 - j], at_z(j))
        pgr[pl.ds(pl.multiple_of(z * 8, 8), 8), :] = pgs[0:8, :]

    def p_end():
        for j in range(1, NZ):
            arrived(pgr.at[pl.ds(pl.multiple_of((z + j) % NZ * 8, 8), 8)],
                    pg_s.at[j - 1], pg_r.at[j - 1])
        for k in range(TOPK):
            pgrad[k:k + 1, :] = jnp.sum(jnp.where(place == place_of(k), pgr[...], 0.0), axis=0,
                                        keepdims=True)

    def each(f, w):
        for r in (1, 3, 2):
            f(w, r)

    ag_hop(0, 1)
    wx_relay(0, 1)
    wx_relay(0, 3)
    ag_hop(1, 1, 0)
    wx_relay(0, 2)
    ag_hop(1, 1, 1)
    p_columns()
    for copy in local:
        copy.wait()
    wy_relay(0, 1)
    wy_relay(0, 3)
    ag_hop(0, 2, 0)
    wy_relay(0, 2)
    ag_hop(0, 2, 1)
    each(wx_relay, 1)
    ag_hop(1, 2, 0)
    each(w_arrive, 0)
    pre_block(0, 4, 0, 2)
    ag_hop(1, 2, 1)
    pre_block(0, 4, 2, 4)
    each(wy_relay, 1)
    ag_hop(0, 3)
    pre_block(4, 3, 0, 2)
    ag_hop(1, 3, 0)
    pre_block(4, 3, 2, 4)
    ag_hop(1, 3, 1)
    each(w_arrive, 1)
    mixed_block(4, 3)
    ag_hop(0, 4)
    pre_block(7, 1)
    mixed_block(7, 1)
    rs_start(0)
    back_block(4, 3)
    ag_hop(1, 4)
    back_block(7, 1)
    rs_step(0, 3)
    input_block(4, 4)
    rs_start(1)
    weight_grad(0)
    mixed_block(0, 4)
    rs_step(0, 2)
    grad_first(0)
    rs_step(1, 3)
    weight_grad(1)
    back_block(0, 4, 0, 3)
    rs_step(0, 1)
    grad_first(1)
    back_block(0, 4, 3, 4)
    input_block(0, 4)
    rs_step(1, 2)
    grad_second(0)
    p_back()
    early = len(started)
    rs_step(1, 1)
    grad_second(1)
    rs_end(0, mixed)
    p_end()
    results = [
        pltpu.make_async_copy(mixed, mixed_out, loc.at[6]),
        pltpu.make_async_copy(pgrad, pgrad_out, loc.at[7]),
        pltpu.make_async_copy(sgrad, sgrad_out, loc.at[8]),
        pltpu.make_async_copy(igrad, igrad_out, loc.at[9]),
    ]
    results[0].start()
    results[1].start()
    grad_end(0)
    grad_end(1)
    results[2].start()
    for copy in started[:early]:
        copy.wait_send()
    rs_end(1, igrad)
    results[3].start()
    for copy in results:
        copy.wait()
    for copy in started[early:]:
        copy.wait_send()


def hand_over(a0, a1, a2, a3, b0, b1, b2, b3):
    for a, b in ((a0, b0), (a1, b1), (a2, b2), (a3, b3)):
        b[...] = a[...]


def body(tokens, expert_ids, probs, first_weight, second_weight, upstream):
    any_spec = pl.BlockSpec(memory_space=pl.ANY)
    vmem_spec = pl.BlockSpec(memory_space=pltpu.VMEM)
    dma = pltpu.SemaphoreType.DMA
    scratch = [
        pltpu.VMEM((TOPK, TOK), jnp.int32),
        pltpu.VMEM((TOPK, TOK), F32),
        pltpu.VMEM((TOK, D), BF16),
        pltpu.VMEM((TOK, D), BF16),
        pltpu.VMEM((1, FF // 8, D), BF16),
        pltpu.VMEM((TOPK, TOK), F32),
        pltpu.VMEM((2, ROWS, D), BF16),
        pltpu.VMEM((D, NX * FF), BF16),
        pltpu.VMEM((NX * FF, D), BF16),
        pltpu.VMEM((ROWS, NX * FF), BF16),
        pltpu.VMEM((ROWS, NX * FF), BF16),
        pltpu.VMEM((ROWS, NX * FF), F32),
        pltpu.VMEM((2, 2, ROWS, HALF), F32),
        pltpu.VMEM((2, 2, 4, 2, TOK, HALF), BF16),
        pltpu.VMEM((2, 2, TOK, HALF), BF16),
        pltpu.VMEM((NZ * 8, TOK), F32),
        pltpu.VMEM((NZ * 8, TOK), F32),
        pltpu.VMEM((TOK, TOK), F32),
        pltpu.VMEM((TOK, TOK), F32),
        pltpu.VMEM((NZ * 8, TOK), F32),
        pltpu.VMEM((NZ * 8, TOK), F32),
        pltpu.VMEM((2, NX, NY, FF // 8, HALF), F32),
        pltpu.VMEM((2, NX, NY, FF // 8, HALF), BF16),
        pltpu.VMEM((2, NX, NY, FF // 8, HALF), BF16),
        pltpu.VMEM((3, NY, FF // 8, HALF), BF16),
        pltpu.VMEM((3, FF // 8, HALF), BF16),
        pltpu.VMEM((3, NX, FF // 8, HALF), BF16),
        pltpu.VMEM((3, FF // 8, HALF), BF16),
        pltpu.VMEM((2, 4, FF // 8, HALF), BF16),
        dma((2, 2, 4, 2)), dma((2, 2, 4, 2)),
        dma((2, 3)), dma((2, 3)),
        dma((2, 3, 2)), dma((2, 3, 2)),
        dma((2, 3, 2)), dma((2, 3, 2)),
        dma((NZ - 1,)), dma((NZ - 1,)),
        dma((NZ - 1,)), dma((NZ - 1,)),
        dma((2, 2, 4, 2)), dma((2, 2, 4, 2)),
        dma((2,)), dma((2,)),
        dma((2, 3)), dma((2, 3)),
        dma((2, 3)), dma((2, 3)),
        dma((10,)),
    ]
    results = pl.pallas_call(
        kernel,
        out_shape=(
            jax.ShapeDtypeStruct((TOK, D), BF16),
            jax.ShapeDtypeStruct((TOK, D), BF16),
            jax.ShapeDtypeStruct((1, FF // 8, D), BF16),
            jax.ShapeDtypeStruct((TOPK, TOK), F32),
        ),
        in_specs=[any_spec] * 6,
        out_specs=(any_spec,) * 4,
        scratch_shapes=scratch,
        compiler_params=pltpu.CompilerParams(
            collective_id=0, has_side_effects=True, vmem_limit_bytes=60 * 1024 * 1024
        ),
        cost_estimate=pl.CostEstimate(
            flops=2 * 5 * ROWS * D * NX * FF, bytes_accessed=8 * 1024 * 1024,
            transcendentals=ROWS * NX * FF,
        ),
    )(tokens, upstream, first_weight, second_weight, expert_ids.T, probs.T)
    mixed, igrad, sgrad, pgrad = pl.pallas_call(
        hand_over,
        out_shape=tuple(jax.ShapeDtypeStruct(r.shape, r.dtype) for r in results),
        in_specs=[vmem_spec] * 4,
        out_specs=(vmem_spec,) * 4,
    )(*results)
    return mixed, igrad, sgrad, pgrad.T


def solution(mesh):
    everything = P(("section", "dp", "expert"), None)
    return jax.shard_map(
        body,
        mesh=mesh,
        in_specs=(everything, everything, everything, P("section", None, None),
                  P("section", None, None), everything),
        out_specs=(everything, everything, P("section", ("dp", "expert"), None), everything),
        check_vma=False,
    )
```
